32 devices in a mesh: grp: 2 (over y), inp: 4 (over z), tblk: 2 (over x), sub: 2 (over core).
Axes of the slice: x: 2, y: 2, z: 4, core: 2. Of those that a mesh axis runs over, the one named last changes fastest.
Arguments:
- voltages: bfloat16 [1024, 393216], P(('grp', 'inp', 'sub'), 'tblk'), parts along dimension 0, may hold values from -6 to 6
- pfb_coeffs: float32 [16, 2048], replicated, may hold values from -1.5 to 1.5
- input_flags: int32 [1024, 192], P(('grp', 'inp', 'sub'), 'tblk'), parts along dimension 0, may hold values 0 or 1
- spec_good: int32 [384], P('grp'), parts along dimension 0, may hold values from 0 to 1, as said below
- chan_map: int32 [512], replicated, may hold values from 0 to 1023, as said below
Outputs:
- visibilities: bfloat16 [1024, 512, 512], P(('grp', 'inp', 'tblk', 'sub')), parts along dimension 0
The draws below stay inside these ranges and needn't reach their ends.
There are 2 independent parts, one for each index of `grp`. The reference program is written for one: setup_inputs(seed, part) draws one part's arguments, and reference() takes and returns one part's arrays. A program takes and returns all parts, laid end to end along the dimension named above; an argument that names none is the same for every part. Nothing has to cross between parts.
Inputs may be any that keep to these rules, and one draw needn't show every extreme that they name: `spec_good`: in each aligned block of 96 spectra between 32 and 64 spectra are kept, and some block keeps exactly 64. `chan_map`: distinct channels; both 0 and 1023 appear.
All inputs are finite; a program needn't handle non-finite values. No bound on the sum of `input_flags` on one device may be relied on, other than what follows from the above.
Results may differ from the reference program's by a relative error of at most 0.0085.
Values may be sent and summed in bfloat16 or wider, within the bound.
No kernel may reach another device: no remote copies, remote signals or barrier semaphores. Data moves between devices by JAX's collectives and lax.ppermute only.
A program may use at most 192 MiB of HBM per device.

```python
import math
import jax
import jax.numpy as jnp
from jax import lax

NIN = 512
NFFT = 2048
NCHAN = 1024
NCHW = 512
TAPS = 16
SPEC_BLK = 96
LIVE = 64
NSPEC = 192
N_TBLK = 2


def block_ranks(block_key):
    return jax.random.permutation(block_key, SPEC_BLK)


def draw_spec_good(key, part):
    key = jax.random.fold_in(key, 11)
    block_total = NSPEC // SPEC_BLK
    count_key, pick_key, order_key = jax.random.split(key, 3)
    counts = jax.random.randint(count_key, (block_total,), LIVE // 2, LIVE + 1)
    fullest = jax.random.randint(pick_key, (), 0, block_total)
    counts = jnp.where(jnp.arange(block_total) == fullest, LIVE, counts)
    order_keys = jax.random.split(order_key, block_total)
    rank_table = jax.vmap(block_ranks)(order_keys)
    return (rank_table < counts[:, None]).astype(jnp.int32).reshape(NSPEC)


def draw_chan_map(key, part):
    key = jax.random.fold_in(key, 23)
    inner_key, place_key = jax.random.split(key)
    middle = 1 + jax.random.permutation(inner_key, NCHAN - 2)[:NCHW - 2]
    listed = jnp.concatenate([jnp.array([0, NCHAN - 1], jnp.int32), middle.astype(jnp.int32)])
    return jax.random.permutation(place_key, listed)


def with_ends(entries, own_key, smallest, top_value):
    index_at = [jax.random.randint(jax.random.fold_in(own_key, axis), (), 0, length) for axis, length in enumerate(entries.shape)]
    widest = entries.shape.index(max(entries.shape))
    next_to = index_at[:widest] + [(index_at[widest] + 1) % entries.shape[widest]] + index_at[widest + 1:]
    return entries.at[tuple(index_at)].set(smallest).at[tuple(next_to)].set(top_value)


def level_of(key, dims, cuts, least, largest):
    def one(position, parts):
        steps = jax.random.uniform(jax.random.fold_in(jax.random.fold_in(key, 6), position), (parts,), jnp.float32, least / len(cuts), largest / len(cuts))
        return jnp.repeat(jnp.exp(steps), dims[position] // parts).reshape((-1,) + (1,) * (len(dims) - position - 1))

    level = one(*cuts[0])
    for cut in cuts[1:]:
        level = level * one(*cut)
    return level


def noise(own_key, extent, spread, most, cuts=(), kind=jnp.bfloat16):
    values = jax.random.normal(own_key, extent, jnp.float32) * spread
    if len(cuts) > 0:
        values = level_of(own_key, extent, cuts, -0.22, 0.18) * values
    return jnp.clip(values, min=-most, max=most).astype(kind)


def setup_inputs(seed: int = 0, part: int = 0) -> dict:
    streams_of = jax.random.split(jax.random.key(seed), 6)
    own_keys = jax.random.split(jax.random.fold_in(streams_of[5], part), 6)
    voltages = noise(own_keys[0], (NIN, NSPEC * NFFT), 1.0, 6.0, ((0, 8), (1, 2)))
    pfb_coeffs = noise(streams_of[1], (TAPS, NFFT), TAPS ** -0.5, 1.5, (), jnp.float32)
    input_flags = with_ends((jax.random.randint(own_keys[2], (NIN, NSPEC), 0, 8) < 7).astype(jnp.int32), jax.random.fold_in(own_keys[2], 1), 0, 1)
    spec_good = draw_spec_good(jax.random.fold_in(jax.random.fold_in(streams_of[5], part), 71), part)
    chan_map = draw_chan_map(jax.random.fold_in(streams_of[5], 71), part)
    return dict(voltages=voltages, pfb_coeffs=pfb_coeffs, input_flags=input_flags, spec_good=spec_good, chan_map=chan_map)


def make_table(channels, frame_len):
    samples = jnp.arange(frame_len, dtype=jnp.int32)
    phase_index = samples[:, None] * channels[None, :].astype(jnp.int32) % frame_len
    angles = phase_index.astype(jnp.float32) * (2.0 * math.pi / frame_len)
    norm_scale = 1.0 / math.sqrt(frame_len)
    return jnp.stack([jnp.cos(angles) * norm_scale, -jnp.sin(angles) * norm_scale], axis=1).astype(jnp.bfloat16)

def correlate_one(spectra_block):
    input_total = spectra_block.shape[0]
    half_width = spectra_block.shape[1] // 2
    rotated = jnp.concatenate([spectra_block[:, half_width:], -spectra_block[:, :half_width]], axis=1)
    stacked = jnp.concatenate([spectra_block, rotated], axis=0)
    products = jnp.dot(stacked, spectra_block.T, preferred_element_type=jnp.float32)
    upper_mask = jnp.arange(input_total)[None, :] >= jnp.arange(input_total)[:, None]
    return jnp.where(upper_mask, products[:input_total], products[input_total:])

def reference(voltages, pfb_coeffs, input_flags, spec_good, chan_map):
    input_total = voltages.shape[0]
    frames = voltages.reshape(input_total, NSPEC, NFFT)
    history = jnp.zeros((input_total, TAPS - 1, NFFT), jnp.bfloat16)
    extended = jnp.concatenate([history, frames], axis=1)
    dft_table = make_table(chan_map, NFFT)
    weights = (input_flags * spec_good[None, :]).astype(jnp.float32)
    live_total = jnp.sum(spec_good).astype(jnp.float32)
    summed_vis = jnp.zeros((NCHW, input_total, input_total), jnp.float32)
    for block_index in range(N_TBLK):
        first_spec = block_index * SPEC_BLK
        summed = jnp.zeros((input_total, SPEC_BLK, NFFT), jnp.float32)
        for tap_index in range(TAPS):
            window_part = extended[:, first_spec + tap_index:first_spec + tap_index + SPEC_BLK, :]
            summed = summed + pfb_coeffs[tap_index][None, None, :] * window_part.astype(jnp.float32)
        filtered = (summed * weights[:, first_spec:first_spec + SPEC_BLK][:, :, None]).astype(jnp.bfloat16)
        spectra = jnp.einsum('isn,nqj->jiqs', filtered.astype(jnp.float32), dft_table.astype(jnp.float32))
        spectra = spectra.astype(jnp.bfloat16).reshape(NCHW, input_total, 2 * SPEC_BLK)
        block_vis = lax.optimization_barrier(lax.map(correlate_one, spectra).astype(jnp.bfloat16))
        summed_vis = summed_vis + block_vis.astype(jnp.float32)
    return (summed_vis / live_total).astype(jnp.bfloat16)
```

```python
import functools
import math

import jax
import jax.numpy as jnp
from jax import lax
from jax.experimental import pallas as pl
from jax.experimental.pallas import tpu as pltpu
from jax.sharding import PartitionSpec as P

MAX_KEPT = 64
STEP = 16
LANES = 128
COLS = 256
VMEM_BYTES = 56 * 1024 * 1024


def passed_along(value, axis, steps):
    count = lax.axis_size(axis)
    initial, last = (max(0, -steps), min(count, count - steps))
    return lax.ppermute(value, axis, [(source, source + steps) for source in range(initial, last)])


def make_table(channels, frame_len):
    scale = 2.0 * math.pi / frame_len
    fine = jnp.arange(LANES, dtype=jnp.int32)
    coarse = jnp.arange(frame_len // LANES, dtype=jnp.int32) * LANES
    fine_angle = (channels[:, None] * fine[None, :] % frame_len).astype(jnp.float32) * scale
    coarse_angle = (channels[:, None] * coarse[None, :] % frame_len).astype(jnp.float32) * scale
    norm_scale = 1.0 / math.sqrt(frame_len)
    parts = (jnp.cos(fine_angle), jnp.sin(fine_angle), jnp.cos(coarse_angle) * norm_scale, jnp.sin(coarse_angle) * norm_scale)
    fine_cos, fine_sin, coarse_cos, coarse_sin = lax.optimization_barrier(parts)
    fine_cos, fine_sin = fine_cos[:, None, :], fine_sin[:, None, :]
    coarse_cos, coarse_sin = coarse_cos[:, :, None], coarse_sin[:, :, None]
    cosine = coarse_cos * fine_cos - coarse_sin * fine_sin
    sine = coarse_sin * fine_cos + coarse_cos * fine_sin
    table = jnp.stack([cosine, -sine]).astype(jnp.bfloat16)
    return table.reshape(2 * channels.shape[0], frame_len)


def kept_rows(good, most):
    length = good.shape[0]
    place = jnp.arange(length, dtype=jnp.int32)
    before = jnp.sum(jnp.where(place[:, None] <= place[None, :], good[:, None], 0), axis=0)
    row = jnp.arange(most, dtype=jnp.int32)
    index = jnp.sum((before[None, :] <= row[:, None]).astype(jnp.int32), axis=1)
    index = jnp.minimum(index, length - 1)
    used = row < jnp.sum(good)
    chosen = (place[None, :] == index[:, None]) & used[:, None]
    return index, chosen


def transform_kernel(slots, with_halo, index_ref, volt_ref, halo_ref, coef_ref, table_ref, weight_ref, out_ref, raw, wide, filt, turn, sems):
    taps, frame_len = coef_ref.shape
    ins = filt.shape[0] // STEP
    first = index_ref[0]
    count = index_ref[STEP - 1] - first + taps

    def each(col, slot, act):
        def body(j, carry):
            extended = first + j
            if with_halo:

                @pl.when(extended < taps - 1)
                def _():
                    begin = pl.multiple_of(extended * frame_len + col * COLS, COLS)
                    act(pltpu.make_async_copy(halo_ref.at[:, pl.ds(begin, COLS)], raw.at[slot, j], sems.at[slot, j]))

            @pl.when(extended >= taps - 1)
            def _():
                begin = pl.multiple_of((extended - (taps - 1)) * frame_len + col * COLS, COLS)
                act(pltpu.make_async_copy(volt_ref.at[:, pl.ds(begin, COLS)], raw.at[slot, j], sems.at[slot, j]))

            return carry

        lax.fori_loop(0, count, body, 0)

    cols = frame_len // COLS
    each(0, 0, lambda c: c.start())

    def column(col, carry):
        slot = lax.rem(col, 2)

        @pl.when(col + 1 < cols)
        def _():
            each(col + 1, 1 - slot, lambda c: c.start())

        each(col, slot, lambda c: c.wait())

        def widen(j, inner):
            wide[j] = raw[slot, j].astype(jnp.float32)
            return inner

        lax.fori_loop(0, count, widen, 0)
        for half in range(COLS // LANES):
            span = pl.ds(half * LANES, LANES)
            here = pl.ds(pl.multiple_of(col * COLS + half * LANES, LANES), LANES)
            coefs = [jnp.broadcast_to(coef_ref[pl.ds(k, 1), here], (8, LANES)) for k in range(taps)]

            def one(r, inner):
                base = index_ref[r] - first
                for group in range(ins // 16):
                    rows = pl.ds(group * 16, 16)
                    total = None
                    for k in range(taps):
                        term = wide[base + k, rows, span].reshape(2, 8, LANES) * coefs[k][None]
                        total = term if total is None else total + term
                    at = pl.ds(pl.multiple_of(r * ins + group * 16, 16), 16)
                    filt[at, here] = total.reshape(16, LANES).astype(jnp.bfloat16)
                return inner

            lax.fori_loop(0, STEP, one, 0)
        return carry

    lax.fori_loop(0, cols, column, 0)

    pairs = STEP * ins // LANES
    per_dot = COLS // LANES

    def multiply(m, carry):
        rows = pl.ds(pl.multiple_of(m * COLS, COLS), COLS)
        for n in range(pairs // per_dot):
            spec = lax.dot_general(
                table_ref[rows, :],
                filt[pl.ds(n * COLS, COLS), :],
                (((1,), (1,)), ((), ())),
                preferred_element_type=jnp.float32,
            )
            for h in range(per_dot):
                b = n * per_dot + h
                turn[pl.ds(pl.multiple_of(b * 2 * slots + m * COLS, COLS), COLS), :] = (
                    spec[:, h * LANES : (h + 1) * LANES] * weight_ref[pl.ds(b, 1), :]
                )
        return carry

    lax.fori_loop(0, 2 * slots // COLS, multiply, 0)

    def corner(j, carry):
        for u in range(8):
            slot = j * 8 + u
            real = turn[pl.ds(slot, pairs, stride=2 * slots), :]
            imag = turn[pl.ds(slots + slot, pairs, stride=2 * slots), :]
            out_ref[slot] = jnp.concatenate([real, imag], axis=0).astype(jnp.bfloat16)
        return carry

    lax.fori_loop(0, slots // 8, corner, 0)


def transform(voltages, halo, coefs, table, index, weight, with_halo):
    ins = voltages.shape[0]
    taps, frame_len = coefs.shape
    slots = table.shape[0] // 2
    frames = voltages.shape[1] // frame_len + taps - 1
    pairs = STEP * ins // LANES
    flops = 2 * STEP * ins * frame_len * 2 * slots
    vmem = pl.BlockSpec(memory_space=pltpu.VMEM)
    hbm = pl.BlockSpec(memory_space=pl.ANY)
    return pl.pallas_call(
        functools.partial(transform_kernel, slots, with_halo),
        out_shape=jax.ShapeDtypeStruct((slots, 2 * pairs, LANES), jnp.bfloat16),
        in_specs=[pl.BlockSpec(memory_space=pltpu.SMEM), hbm, hbm, vmem, vmem, vmem],
        out_specs=vmem,
        scratch_shapes=[
            pltpu.VMEM((2, frames, ins, COLS), jnp.bfloat16),
            pltpu.VMEM((frames, ins, COLS), jnp.float32),
            pltpu.VMEM((STEP * ins, frame_len), jnp.bfloat16),
            pltpu.VMEM((pairs * 2 * slots, LANES), jnp.float32),
            pltpu.SemaphoreType.DMA((2, frames)),
        ],
        compiler_params=pltpu.CompilerParams(vmem_limit_bytes=VMEM_BYTES),
        cost_estimate=pl.CostEstimate(flops=4 * flops, bytes_accessed=12 * 2**20, transcendentals=0),
        name="filter_transform",
    )(index, voltages, halo, coefs, table, weight)


def correlate_kernel(blocks, chips, cores, pieces, *refs):
    scale_ref, refs = refs[0], refs[1:]
    part_refs = refs[:pieces]
    out_ref, straight, turned = refs[-3:]
    ins = LANES // cores
    total = straight.shape[1]
    half_depth = part_refs[0].shape[-2] // 2
    low = lax.broadcasted_iota(jnp.int32, (half_depth, LANES), 1) < ins
    for chip in range(chips):
        lanes = pl.ds(chip * LANES, LANES)
        place = 0
        for block in range(blocks):
            sources = [(chip * blocks + block) * cores + core for core in range(cores)]
            for part in part_refs:
                for step in range(part.shape[1]):
                    one, two = (part[source, step, 0].astype(jnp.float32) for source in sources)
                    one = (one[:half_depth], one[half_depth:])
                    two = (two[:half_depth], two[half_depth:])
                    first = [jnp.where(low, a, pltpu.roll(b, ins, 1)) for a, b in zip(one, two)]
                    second = [jnp.where(low, pltpu.roll(a, ins, 1), b) for a, b in zip(one, two)]
                    for real, imag in (first, second):
                        rows = pl.ds(place, 2 * half_depth)
                        straight[rows, lanes] = jnp.concatenate([real, imag], axis=0).astype(jnp.bfloat16)
                        turned[rows, lanes] = jnp.concatenate([-imag, real], axis=0).astype(jnp.bfloat16)
                        place += 2 * half_depth
    left = straight[...].T
    scale = scale_ref[0]
    half = total // 2

    def product(a, ref, b):
        return jnp.dot(left[a * half : (a + 1) * half], ref[:, b * half : (b + 1) * half], preferred_element_type=jnp.float32) * scale

    upper = lax.broadcasted_iota(jnp.int32, (half, half), 1) >= lax.broadcasted_iota(jnp.int32, (half, half), 0)
    for a in range(2):
        here = pl.ds(a * half, half)
        both = jnp.where(upper, product(a, straight, a), product(a, turned, a))
        out_ref[0, here, here] = both.astype(out_ref.dtype)
    out_ref[0, :half, half:] = product(0, straight, 1).astype(out_ref.dtype)
    out_ref[0, half:, :half] = product(1, turned, 0).astype(out_ref.dtype)


def correlate(scale, parts, into, first, own, blocks, chips, cores):
    count = min(part.shape[2] - begin for part, begin in parts)
    sources = blocks * chips * cores
    total = chips * LANES
    depth = blocks * cores * sum(part.shape[1] * part.shape[3] for part, _ in parts)

    def spec(part, begin):
        return pl.BlockSpec((sources, part.shape[1], 1) + part.shape[3:], lambda c: (0, 0, c + begin, 0, 0))

    arrays = [part for part, _ in parts]
    in_specs = [pl.BlockSpec(memory_space=pltpu.SMEM)] + [spec(*pair) for pair in parts]
    operands = [scale] + arrays
    aliases = {}
    kernel = functools.partial(correlate_kernel, blocks, chips, cores, len(parts))
    if into is not None:
        aliases = {len(operands): 0}
        operands.append(into)
        in_specs.append(pl.BlockSpec(memory_space=pl.ANY))
    return pl.pallas_call(
        kernel,
        grid=(count,),
        out_shape=jax.ShapeDtypeStruct((own, total, total), jnp.bfloat16),
        in_specs=in_specs,
        out_specs=pl.BlockSpec((1, total, total), lambda c: (c + first, 0, 0)),
        scratch_shapes=[pltpu.VMEM((depth, total), jnp.bfloat16)] * 2,
        input_output_aliases=aliases,
        compiler_params=pltpu.CompilerParams(vmem_limit_bytes=VMEM_BYTES),
        cost_estimate=pl.CostEstimate(
            flops=count * 8 * total * total * depth, bytes_accessed=count * 3 * total * total, transcendentals=0
        ),
        name="correlate",
    )(*operands)


def make_plain_table(channels, frame_len):
    samples = jnp.arange(frame_len, dtype=jnp.int32)
    phase_index = samples[:, None] * channels[None, :] % frame_len
    angles = phase_index.astype(jnp.float32) * (2.0 * math.pi / frame_len)
    norm_scale = 1.0 / math.sqrt(frame_len)
    return jnp.stack([jnp.cos(angles) * norm_scale, -jnp.sin(angles) * norm_scale], axis=1).astype(
        jnp.bfloat16
    )


def correlate_one(spectra_block):
    input_total = spectra_block.shape[0]
    half_width = spectra_block.shape[1] // 2
    rotated = jnp.concatenate(
        [spectra_block[:, half_width:], -spectra_block[:, :half_width]], axis=1
    )
    stacked = jnp.concatenate([spectra_block, rotated], axis=0)
    products = jnp.dot(stacked, spectra_block.T, preferred_element_type=jnp.float32)
    upper_mask = jnp.arange(input_total)[None, :] >= jnp.arange(input_total)[:, None]
    return jnp.where(upper_mask, products[:input_total], products[input_total:])


def rounded(values):
    return lax.optimization_barrier(values.astype(jnp.bfloat16)).astype(jnp.float32)


def local_plain(voltages, pfb_coeffs, input_flags, spec_good, chan_map):
    tap_count, frame_len = pfb_coeffs.shape
    local_inputs, block_len = input_flags.shape
    frames = voltages.reshape(local_inputs, block_len, frame_len)
    earlier = passed_along(frames[:, block_len - tap_count + 1 :, :], "tblk", 1)
    extended = jnp.concatenate([earlier, frames], axis=1)
    summed = jnp.zeros((local_inputs, block_len, frame_len), jnp.float32)
    for tap_index in range(tap_count):
        window_part = extended[:, tap_index : tap_index + block_len, :]
        summed = summed + pfb_coeffs[tap_index][None, None, :] * window_part.astype(jnp.float32)
    block_index = lax.axis_index("tblk")
    good_here = lax.dynamic_slice_in_dim(spec_good, block_index * block_len, block_len)
    weights = input_flags * good_here[None, :]
    filtered = (summed * weights.astype(jnp.float32)[:, :, None]).astype(jnp.bfloat16)
    inp_count = lax.axis_size("inp")
    tblk_count = lax.axis_size("tblk")
    sub_count = lax.axis_size("sub")
    chan_total = chan_map.shape[0]
    per_owner = chan_total // (inp_count * tblk_count * sub_count)
    live_total = jnp.sum(spec_good).astype(jnp.float32)
    slot_order = jnp.arange(chan_total).reshape(inp_count, tblk_count, sub_count, per_owner)
    slot_order = slot_order.transpose(0, 2, 1, 3).reshape(chan_total)
    dft_table = make_plain_table(chan_map[slot_order], frame_len)
    spectra = jnp.einsum("isn,nqj->jiqs", filtered, dft_table, preferred_element_type=jnp.float32)
    spectra = spectra.astype(jnp.bfloat16).reshape(chan_total, local_inputs, -1)
    turned = lax.all_to_all(spectra, ("inp", "sub"), split_axis=0, concat_axis=1, tiled=True)
    summed_vis = lax.psum_scatter(
        rounded(lax.map(correlate_one, turned)).astype(jnp.bfloat16),
        "tblk",
        scatter_dimension=0,
        tiled=True,
    ).astype(jnp.float32)
    return (summed_vis / live_total).astype(jnp.bfloat16)


def local(voltages, pfb_coeffs, input_flags, spec_good, chan_map):
    taps, frame_len = pfb_coeffs.shape
    ins, block_len = input_flags.shape
    chips, blocks, cores = (lax.axis_size(axis) for axis in ("inp", "tblk", "sub"))
    owners = chips * blocks * cores
    slots = chan_map.shape[0]
    own = slots // owners
    if ins * cores != LANES or own % 2 or ins % 16:
        return local_plain(voltages, pfb_coeffs, input_flags, spec_good, chan_map)
    halo = passed_along(voltages[:, (block_len - taps + 1) * frame_len :], "tblk", 1)
    good = lax.dynamic_slice_in_dim(spec_good, lax.axis_index("tblk") * block_len, block_len)
    index, chosen = kept_rows(good, MAX_KEPT)
    weight = jnp.dot(
        chosen.astype(jnp.bfloat16), input_flags.astype(jnp.bfloat16).T, preferred_element_type=jnp.float32
    ).reshape(MAX_KEPT * ins // LANES, LANES)
    table = make_table(chan_map, frame_len)
    pairs = STEP * ins // LANES
    scale = (1.0 / jnp.sum(spec_good).astype(jnp.float32)).reshape(1)

    def chunk(step):
        done = transform(
            voltages,
            halo if step == 0 else voltages,
            pfb_coeffs,
            table,
            index[step * STEP : (step + 1) * STEP],
            weight[step * pairs : (step + 1) * pairs],
            step == 0,
        )
        return done.reshape(owners, 1, own, 2 * pairs, LANES)

    def turn(piece):
        return lax.all_to_all(piece, ("inp", "tblk", "sub"), split_axis=0, concat_axis=0, tiled=True)

    early = turn(chunk(1))
    middle = turn(jnp.concatenate([chunk(2), chunk(3)], axis=1))
    last = chunk(0)
    cuts = 2
    each = own // cuts
    out = None
    for cut in range(cuts):
        tail = turn(last[:, :, cut * each : (cut + 1) * each])
        out = correlate(
            scale, [(early, cut * each), (middle, cut * each), (tail, 0)], out, cut * each, own, blocks, chips, cores
        )
    return out


def solution(mesh):
    return jax.shard_map(
        local,
        mesh=mesh,
        in_specs=(
            P(("grp", "inp", "sub"), "tblk"),
            P(),
            P(("grp", "inp", "sub"), "tblk"),
            P("grp"),
            P(),
        ),
        out_specs=P(("grp", "inp", "tblk", "sub"), None, None),
        check_vma=False,
    )
```

```python
import functools
import math

import jax
import jax.numpy as jnp
from jax import lax
from jax.experimental import pallas as pl
from jax.experimental.pallas import tpu as pltpu
from jax.sharding import PartitionSpec as P

MAX_KEPT = 64
STEP = 16
LANES = 128
COLS = 256
AHEAD = 8
VMEM_BYTES = 56 * 1024 * 1024


def passed_along(value, axis, steps):
    count = lax.axis_size(axis)
    initial, last = (max(0, -steps), min(count, count - steps))
    return lax.ppermute(value, axis, [(source, source + steps) for source in range(initial, last)])


def fill_table(chan_ref, table_ref, frame_len):
    slots = chan_ref.shape[0]
    scale = 2.0 * math.pi / frame_len
    norm_scale = 1.0 / math.sqrt(frame_len)

    def block(step, carry):
        rows = pl.ds(pl.multiple_of(step * 64, 64), 64)
        lane = lax.broadcasted_iota(jnp.int32, (64, LANES), 1)
        channels = chan_ref[rows, :]
        fine = lax.rem(channels * lane, frame_len).astype(jnp.float32) * scale
        coarse = lax.rem(channels * lane * LANES, frame_len).astype(jnp.float32) * scale
        fine_cos, fine_sin = jnp.cos(fine), jnp.sin(fine)
        coarse_cos, coarse_sin = jnp.cos(coarse) * norm_scale, jnp.sin(coarse) * norm_scale
        for part in range(frame_len // LANES):
            span = pl.ds(part * LANES, LANES)
            cosine, sine = coarse_cos[:, part : part + 1], coarse_sin[:, part : part + 1]
            below = pl.ds(pl.multiple_of(slots + step * 64, 64), 64)
            table_ref[rows, span] = (cosine * fine_cos - sine * fine_sin).astype(table_ref.dtype)
            table_ref[below, span] = -(sine * fine_cos + cosine * fine_sin).astype(table_ref.dtype)
        return carry

    lax.fori_loop(0, slots // 64, block, 0)


def transform_kernel(row_first, rows, with_halo, starts, *refs):
    place_ref, good_ref, flag_ref, volt_ref, coef_ref, halo_ref, table_in, _, *refs = refs
    if starts:
        out_ref, table_ref, last_ref, *refs = refs
    else:
        out_ref, *refs = refs
        table_ref = table_in
    index_ref, raw, wide, hot, weight, filt, turn, sems, last_sem = refs
    taps, frame_len = coef_ref.shape
    ins, block_len = flag_ref.shape
    slots = table_ref.shape[0] // 2
    ring, ahead = wide.shape[0], raw.shape[0]
    pairs = rows * ins // LANES

    def note(s, carry):
        seen, latest = carry
        keep = good_ref[place_ref[0] * block_len + s] > 0
        mine = keep & (seen >= row_first) & (seen < row_first + rows)

        @pl.when(mine)
        def _():
            index_ref[seen - row_first] = s

        return seen + keep.astype(jnp.int32), jnp.where(mine, s, latest)

    seen, latest = lax.fori_loop(0, block_len, note, (jnp.int32(0), jnp.int32(block_len - 1)))
    used = jnp.clip(seen - row_first, 0, rows)

    def rest(r, carry):
        index_ref[r] = latest
        return carry

    lax.fori_loop(used, rows, rest, 0)
    first = index_ref[0]
    end = index_ref[rows - 1] + taps

    def on_copy(extended, act):
        slot = lax.rem(extended, ahead)

        def one(ref, frame):
            begin = pl.multiple_of(frame * frame_len, frame_len)
            act(pltpu.make_async_copy(ref.at[:, pl.ds(begin, frame_len)], raw.at[slot], sems.at[slot]))

        if with_halo:

            @pl.when(extended < taps - 1)
            def _():
                one(halo_ref, extended)

        @pl.when(extended >= taps - 1)
        def _():
            one(volt_ref, extended - (taps - 1))

    def fetch(extended):
        @pl.when(extended < end)
        def _():
            on_copy(extended, lambda c: c.start())

    for k in range(ahead):
        fetch(first + k)
    if starts:
        pass_on = pltpu.make_async_copy(
            volt_ref.at[:, pl.ds((block_len - taps + 1) * frame_len, (taps - 1) * frame_len)], last_ref, last_sem
        )
        pass_on.start()
        fill_table(table_in, table_ref, frame_len)

    spectrum = lax.broadcasted_iota(jnp.int32, (1, block_len), 1)
    for r in range(rows):
        chosen = (spectrum == index_ref[r]) & (jnp.int32(r) < used)
        hot[pl.ds((r % 2) * (rows // 2) + r // 2, 1), :] = chosen.astype(jnp.float32)
    flags = flag_ref[...].astype(jnp.float32)
    weights = lax.dot_general(hot[...], flags, (((1,), (1,)), ((), ())), preferred_element_type=jnp.float32)
    weight[...] = jnp.concatenate([weights[: rows // 2], weights[rows // 2 :]], axis=1)

    def take(extended, carry):
        on_copy(extended, lambda c: c.wait())
        to, came = lax.rem(extended, ring), lax.rem(extended, ahead)
        for col in range(frame_len // LANES):
            wide[to, col] = raw[came, :, col * LANES : (col + 1) * LANES].astype(jnp.float32)
        fetch(extended + ahead)
        return carry

    def row(r, have):
        base = index_ref[r]
        lax.fori_loop(have, base + taps, take, 0)
        places = [lax.rem(base + k, ring) for k in range(taps)]
        at = pl.ds(pl.multiple_of(r * ins, ins), ins)
        for col in range(frame_len // LANES):
            here = pl.ds(col * LANES, LANES)
            total = None
            for k in range(taps):
                term = wide[places[k], col] * coef_ref[pl.ds(k, 1), here]
                total = term if total is None else total + term
            filt[at, here] = total.astype(jnp.bfloat16)
        return jnp.maximum(have, base + taps)

    lax.fori_loop(0, rows, row, first)

    per_dot = COLS // LANES

    def multiply(m, carry):
        here = pl.ds(pl.multiple_of(m * COLS, COLS), COLS)
        for n in range(pairs // per_dot):
            spec = lax.dot_general(
                table_ref[here, :],
                filt[pl.ds(n * COLS, COLS), :],
                (((1,), (1,)), ((), ())),
                preferred_element_type=jnp.float32,
            )
            for h in range(per_dot):
                b = n * per_dot + h
                turn[pl.ds(pl.multiple_of(b * 2 * slots + m * COLS, COLS), COLS), :] = (
                    spec[:, h * LANES : (h + 1) * LANES] * weight[pl.ds(b, 1), :]
                )
        return carry

    lax.fori_loop(0, 2 * slots // COLS, multiply, 0)

    def corner(j, carry):
        for u in range(8):
            slot = j * 8 + u
            real = turn[pl.ds(slot, pairs, stride=2 * slots), :]
            imag = turn[pl.ds(slots + slot, pairs, stride=2 * slots), :]
            out_ref[slot] = jnp.concatenate([real, imag], axis=0).astype(jnp.bfloat16)
        return carry

    lax.fori_loop(0, slots // 8, corner, 0)
    if starts:
        pass_on.wait()


def transform(place, spec_good, input_flags, voltages, coefs, halo, table, after, row_first, rows):
    ins, block_len = input_flags.shape
    taps, frame_len = coefs.shape
    starts = table.ndim == 2 and table.shape[1] == 1
    slots = table.shape[0] if starts else table.shape[0] // 2
    pairs = rows * ins // LANES
    flops = 2 * rows * ins * frame_len * 2 * slots
    smem = pl.BlockSpec(memory_space=pltpu.SMEM)
    vmem = pl.BlockSpec(memory_space=pltpu.VMEM)
    hbm = pl.BlockSpec(memory_space=pl.ANY)
    out_shape = [jax.ShapeDtypeStruct((slots, 2 * pairs, LANES), jnp.bfloat16)]
    out_specs = [vmem]
    if starts:
        out_shape.append(jax.ShapeDtypeStruct((2 * slots, frame_len), jnp.bfloat16))
        out_shape.append(jax.ShapeDtypeStruct((ins, (taps - 1) * frame_len), jnp.bfloat16))
        out_specs += [vmem, hbm]
    return pl.pallas_call(
        functools.partial(transform_kernel, row_first, rows, halo is not None, starts),
        out_shape=out_shape,
        in_specs=[smem, smem, vmem, hbm, vmem, hbm, vmem, hbm],
        out_specs=out_specs,
        scratch_shapes=[
            pltpu.SMEM((rows,), jnp.int32),
            pltpu.VMEM((AHEAD, ins, frame_len), jnp.bfloat16),
            pltpu.VMEM((taps, frame_len // LANES, ins, LANES), jnp.float32),
            pltpu.VMEM((rows, block_len), jnp.float32),
            pltpu.VMEM((pairs, LANES), jnp.float32),
            pltpu.VMEM((rows * ins, frame_len), jnp.bfloat16),
            pltpu.VMEM((pairs * 2 * slots, LANES), jnp.float32),
            pltpu.SemaphoreType.DMA((AHEAD,)),
            pltpu.SemaphoreType.DMA,
        ],
        compiler_params=pltpu.CompilerParams(vmem_limit_bytes=VMEM_BYTES),
        cost_estimate=pl.CostEstimate(flops=4 * flops, bytes_accessed=12 * 2**20, transcendentals=0),
        name="filter_transform",
    )(place, spec_good, input_flags, voltages, coefs, voltages if halo is None else halo, table, voltages if after is None else after)


def correlate_kernel(blocks, chips, cores, pieces, *refs):
    scale_ref, refs = refs[0], refs[1:]
    part_refs = refs[:pieces]
    out_ref, straight, turned = refs[-3:]
    ins = LANES // cores
    total = straight.shape[1]
    for chip in range(chips):
        lanes = pl.ds(chip * LANES, LANES)
        place = 0
        for block in range(blocks):
            sources = [(chip * blocks + block) * cores + core for core in range(cores)]
            for part in part_refs:
                depth = part.shape[2]
                half_depth = depth // 2
                one, two = (part[source, 0].astype(jnp.float32) for source in sources)
                low = lax.broadcasted_iota(jnp.int32, (depth, LANES), 1) < ins
                first = jnp.where(low, one, pltpu.roll(two, ins, 1))
                second = jnp.where(low, pltpu.roll(one, ins, 1), two)
                for both in (first, second):
                    rows = pl.ds(place, depth)
                    straight[rows, lanes] = both.astype(jnp.bfloat16)
                    turned[rows, lanes] = jnp.concatenate([-both[half_depth:], both[:half_depth]], axis=0).astype(jnp.bfloat16)
                    place += depth
    left = straight[...].T
    scale = scale_ref[0]
    half = total // 2

    def product(a, ref, b):
        return jnp.dot(left[a * half : (a + 1) * half], ref[:, b * half : (b + 1) * half], preferred_element_type=jnp.float32) * scale

    upper = lax.broadcasted_iota(jnp.int32, (half, half), 1) >= lax.broadcasted_iota(jnp.int32, (half, half), 0)
    for a in range(2):
        here = pl.ds(a * half, half)
        both = jnp.where(upper, product(a, straight, a), product(a, turned, a))
        out_ref[0, here, here] = both.astype(out_ref.dtype)
    out_ref[0, :half, half:] = product(0, straight, 1).astype(out_ref.dtype)
    out_ref[0, half:, :half] = product(1, turned, 0).astype(out_ref.dtype)


def correlate(scale, parts, into, first, own, blocks, chips, cores):
    count = min(part.shape[1] - begin for part, begin in parts)
    sources = blocks * chips * cores
    total = chips * LANES
    depth = blocks * cores * sum(part.shape[2] for part, _ in parts)

    def spec(part, begin):
        return pl.BlockSpec((sources, 1) + part.shape[2:], lambda c: (0, c + begin, 0, 0))

    arrays = [part for part, _ in parts]
    in_specs = [pl.BlockSpec(memory_space=pltpu.SMEM)] + [spec(*pair) for pair in parts]
    operands = [scale] + arrays
    aliases = {}
    kernel = functools.partial(correlate_kernel, blocks, chips, cores, len(parts))
    if into is not None:
        aliases = {len(operands): 0}
        operands.append(into)
        in_specs.append(pl.BlockSpec(memory_space=pl.ANY))
    return pl.pallas_call(
        kernel,
        grid=(count,),
        out_shape=jax.ShapeDtypeStruct((own, total, total), jnp.bfloat16),
        in_specs=in_specs,
        out_specs=pl.BlockSpec((1, total, total), lambda c: (c + first, 0, 0)),
        scratch_shapes=[pltpu.VMEM((depth, total), jnp.bfloat16)] * 2,
        input_output_aliases=aliases,
        compiler_params=pltpu.CompilerParams(vmem_limit_bytes=VMEM_BYTES),
        cost_estimate=pl.CostEstimate(
            flops=count * 8 * total * total * depth, bytes_accessed=count * 3 * total * total, transcendentals=0
        ),
        name="correlate",
    )(*operands)


def make_plain_table(channels, frame_len):
    samples = jnp.arange(frame_len, dtype=jnp.int32)
    phase_index = samples[:, None] * channels[None, :] % frame_len
    angles = phase_index.astype(jnp.float32) * (2.0 * math.pi / frame_len)
    norm_scale = 1.0 / math.sqrt(frame_len)
    return jnp.stack([jnp.cos(angles) * norm_scale, -jnp.sin(angles) * norm_scale], axis=1).astype(
        jnp.bfloat16
    )


def correlate_one(spectra_block):
    input_total = spectra_block.shape[0]
    half_width = spectra_block.shape[1] // 2
    rotated = jnp.concatenate(
        [spectra_block[:, half_width:], -spectra_block[:, :half_width]], axis=1
    )
    stacked = jnp.concatenate([spectra_block, rotated], axis=0)
    products = jnp.dot(stacked, spectra_block.T, preferred_element_type=jnp.float32)
    upper_mask = jnp.arange(input_total)[None, :] >= jnp.arange(input_total)[:, None]
    return jnp.where(upper_mask, products[:input_total], products[input_total:])


def rounded(values):
    return lax.optimization_barrier(values.astype(jnp.bfloat16)).astype(jnp.float32)


def local_plain(voltages, pfb_coeffs, input_flags, spec_good, chan_map):
    tap_count, frame_len = pfb_coeffs.shape
    local_inputs, block_len = input_flags.shape
    frames = voltages.reshape(local_inputs, block_len, frame_len)
    earlier = passed_along(frames[:, block_len - tap_count + 1 :, :], "tblk", 1)
    extended = jnp.concatenate([earlier, frames], axis=1)
    summed = jnp.zeros((local_inputs, block_len, frame_len), jnp.float32)
    for tap_index in range(tap_count):
        window_part = extended[:, tap_index : tap_index + block_len, :]
        summed = summed + pfb_coeffs[tap_index][None, None, :] * window_part.astype(jnp.float32)
    block_index = lax.axis_index("tblk")
    good_here = lax.dynamic_slice_in_dim(spec_good, block_index * block_len, block_len)
    weights = input_flags * good_here[None, :]
    filtered = (summed * weights.astype(jnp.float32)[:, :, None]).astype(jnp.bfloat16)
    inp_count = lax.axis_size("inp")
    tblk_count = lax.axis_size("tblk")
    sub_count = lax.axis_size("sub")
    chan_total = chan_map.shape[0]
    per_owner = chan_total // (inp_count * tblk_count * sub_count)
    live_total = jnp.sum(spec_good).astype(jnp.float32)
    slot_order = jnp.arange(chan_total).reshape(inp_count, tblk_count, sub_count, per_owner)
    slot_order = slot_order.transpose(0, 2, 1, 3).reshape(chan_total)
    dft_table = make_plain_table(chan_map[slot_order], frame_len)
    spectra = jnp.einsum("isn,nqj->jiqs", filtered, dft_table, preferred_element_type=jnp.float32)
    spectra = spectra.astype(jnp.bfloat16).reshape(chan_total, local_inputs, -1)
    turned = lax.all_to_all(spectra, ("inp", "sub"), split_axis=0, concat_axis=1, tiled=True)
    summed_vis = lax.psum_scatter(
        rounded(lax.map(correlate_one, turned)).astype(jnp.bfloat16),
        "tblk",
        scatter_dimension=0,
        tiled=True,
    ).astype(jnp.float32)
    return (summed_vis / live_total).astype(jnp.bfloat16)


def local(voltages, pfb_coeffs, input_flags, spec_good, chan_map):
    taps, frame_len = pfb_coeffs.shape
    ins, block_len = input_flags.shape
    chips, blocks, cores = (lax.axis_size(axis) for axis in ("inp", "tblk", "sub"))
    owners = chips * blocks * cores
    slots = chan_map.shape[0]
    own = slots // owners
    if ins * cores != LANES or own % 4 or ins % 16 or slots % 64:
        return local_plain(voltages, pfb_coeffs, input_flags, spec_good, chan_map)
    place = lax.axis_index("tblk").astype(jnp.int32).reshape(1)
    scale = (1.0 / jnp.sum(spec_good).astype(jnp.float32)).reshape(1)

    def chunk(row_first, rows, halo, table, after):
        done, *more = transform(
            place, spec_good, input_flags, voltages, pfb_coeffs, halo, table, after, row_first, rows
        )
        return [done.reshape(owners, own, *done.shape[1:])] + more

    def turn(piece):
        return lax.all_to_all(piece, ("inp", "tblk", "sub"), split_axis=0, concat_axis=0, tiled=True)

    early, table, last_frames = chunk(STEP, STEP, None, chan_map.reshape(slots, 1), None)
    turned = [(turn(early), 0)]
    halo = passed_along(last_frames, "tblk", 1)
    (middle,) = chunk(2 * STEP, 2 * STEP, None, table, early)
    turned.append((turn(middle), 0))
    (late,) = chunk(0, STEP, halo, table, middle)
    out = None
    for begin, end in ((0, own * 3 // 4), (own * 3 // 4, own)):
        tail = turn(late[:, begin:end])
        parts = [(part, begin) for part, _ in turned] + [(tail, 0)]
        out = correlate(scale, parts, out, begin, own, blocks, chips, cores)
    return out


def solution(mesh):
    return jax.shard_map(
        local,
        mesh=mesh,
        in_specs=(
            P(("grp", "inp", "sub"), "tblk"),
            P(),
            P(("grp", "inp", "sub"), "tblk"),
            P("grp"),
            P(),
        ),
        out_specs=P(("grp", "inp", "tblk", "sub"), None, None),
        check_vma=False,
    )
```

```python
import functools
import math

import jax
import jax.numpy as jnp
from jax import lax
from jax.experimental import pallas as pl
from jax.experimental.pallas import tpu as pltpu
from jax.sharding import PartitionSpec as P

MAX_KEPT = 64
STEP = 16
LANES = 128
COLS = 256
SLOTS = 4
BLOCKS = 2
AHEAD = 8
VMEM_BYTES = 56 * 1024 * 1024


def passed_along(value, axis, steps):
    count = lax.axis_size(axis)
    initial, last = (max(0, -steps), min(count, count - steps))
    return lax.ppermute(value, axis, [(source, source + steps) for source in range(initial, last)])


def turn_of(places, frame_len):
    quarter = frame_len // 4
    turns = (places + quarter // 2) // quarter
    angle = (places - turns * quarter).astype(jnp.float32) * (2.0 * math.pi / frame_len)
    square = angle * angle
    sine = angle * (1.0 + square * (-1.0 / 6 + square * (1.0 / 120 + square * (-1.0 / 5040 + square * (1.0 / 362880)))))
    cosine = 1.0 + square * (-0.5 + square * (1.0 / 24 + square * (-1.0 / 720 + square * (1.0 / 40320))))
    odd = (turns == 1) | (turns == 3)
    first, second = jnp.where(odd, sine, cosine), jnp.where(odd, cosine, sine)
    return (
        jnp.where((turns == 1) | (turns == 2), -first, first),
        jnp.where((turns == 2) | (turns == 3), -second, second),
    )


def fill_table(chan_ref, table_ref, frame_len):
    slots = chan_ref.shape[0]
    norm_scale = 1.0 / math.sqrt(frame_len)

    def block(step, carry):
        rows = pl.ds(pl.multiple_of(step * 64, 64), 64)
        lane = lax.broadcasted_iota(jnp.int32, (64, LANES), 1)
        channels = chan_ref[rows, :]
        fine_cos, fine_sin = turn_of(lax.rem(channels * lane, frame_len), frame_len)
        coarse_cos, coarse_sin = turn_of(lax.rem(channels * lane * LANES, frame_len), frame_len)
        coarse_cos, coarse_sin = coarse_cos * norm_scale, coarse_sin * norm_scale
        for part in range(frame_len // LANES):
            span = pl.ds(part * LANES, LANES)
            cosine, sine = coarse_cos[:, part : part + 1], coarse_sin[:, part : part + 1]
            below = pl.ds(pl.multiple_of(slots + step * 64, 64), 64)
            table_ref[rows, span] = (cosine * fine_cos - sine * fine_sin).astype(table_ref.dtype)
            table_ref[below, span] = -(sine * fine_cos + cosine * fine_sin).astype(table_ref.dtype)
        return carry

    lax.fori_loop(0, slots // 64, block, 0)


def transform_kernel(row_first, rows, nexts, starts, owners, cores, *refs):
    place_ref, good_ref, flag_ref, volt_ref, coef_ref, table_in, _, *refs = refs
    if starts:
        table_out, *refs = refs
    out_refs = refs[: BLOCKS if owners else 1]
    index_ref, raw, wide, hot, weight, filt, turn, table, sems, table_sem = refs[len(out_refs) :]
    taps, frame_len = coef_ref.shape
    ins = flag_ref.shape[0]
    blocks = BLOCKS
    block_len = good_ref.shape[0] // BLOCKS
    slots = table.shape[0] // 2
    ring, ahead = wide.shape[0], raw.shape[0]
    pairs = rows * ins // LANES
    block = place_ref[0]

    if starts:
        move = pltpu.make_async_copy(table, table_out, table_sem)
    else:
        move = pltpu.make_async_copy(table_in, table, table_sem)
        move.start()

    def note(s, carry):
        seen, latest = carry
        if nexts:
            keep = (block + 1 < blocks) & (good_ref[jnp.minimum(block + 1, blocks - 1) * block_len + s] > 0)
        else:
            keep = good_ref[block * block_len + s] > 0
        mine = keep & (seen >= row_first) & (seen < row_first + rows)
        spectrum = s + block_len if nexts else s

        @pl.when(mine)
        def _():
            index_ref[seen - row_first] = spectrum

        return seen + keep.astype(jnp.int32), jnp.where(mine, spectrum, latest)

    span = taps - 1 if nexts else block_len
    seen, latest = lax.fori_loop(0, span, note, (jnp.int32(0), jnp.int32(block_len - 1)))
    used = jnp.clip(seen - row_first, 0, rows)

    def rest(r, carry):
        index_ref[r] = latest
        return carry

    lax.fori_loop(used, rows, rest, 0)
    first = index_ref[0]
    end = index_ref[rows - 1] + taps

    def inside(extended):
        return (extended >= taps - 1) & (extended < taps - 1 + block_len)

    def on_copy(extended):
        slot = lax.rem(extended, ahead)
        begin = pl.multiple_of((extended - (taps - 1)) * frame_len, frame_len)
        return pltpu.make_async_copy(volt_ref.at[:, pl.ds(begin, frame_len)], raw.at[slot], sems.at[slot])

    def fetch(extended):
        @pl.when((extended < end) & inside(extended))
        def _():
            on_copy(extended).start()

    for k in range(ahead):
        fetch(first + k)
    if starts:
        fill_table(table_in, table, frame_len)
        move.start()

    spectrum = lax.broadcasted_iota(jnp.int32, (1, hot.shape[1]), 1) + (block_len if nexts else 0)
    for r in range(rows):
        chosen = (spectrum == index_ref[r]) & (jnp.int32(r) < used)
        hot[pl.ds((r % 2) * (rows // 2) + r // 2, 1), :] = chosen.astype(jnp.float32)
    flags = flag_ref[...].astype(jnp.float32)
    weights = lax.dot_general(hot[...], flags, (((1,), (1,)), ((), ())), preferred_element_type=jnp.float32)
    weight[...] = jnp.concatenate([weights[: rows // 2], weights[rows // 2 :]], axis=1)

    def take(extended, carry):
        to, came = lax.rem(extended, ring), lax.rem(extended, ahead)

        @pl.when(inside(extended))
        def _():
            on_copy(extended).wait()
            for col in range(frame_len // LANES):
                wide[to, col] = raw[came, :, col * LANES : (col + 1) * LANES].astype(jnp.float32)

        @pl.when(jnp.logical_not(inside(extended)))
        def _():
            wide[to] = jnp.zeros(wide.shape[1:], wide.dtype)

        fetch(extended + ahead)
        return carry

    def filter_row(r, have):
        base = index_ref[r]
        lax.fori_loop(have, base + taps, take, 0)
        places = [lax.rem(base + k, ring) for k in range(taps)]
        at = pl.ds(pl.multiple_of(r * ins, ins), ins)
        for col in range(frame_len // LANES):
            here = pl.ds(col * LANES, LANES)
            total = None
            for k in range(taps):
                term = wide[places[k], col] * coef_ref[pl.ds(k, 1), here]
                total = term if total is None else total + term
            filt[at, here] = total.astype(jnp.bfloat16)
        return jnp.maximum(have, base + taps)

    lax.fori_loop(0, rows, filter_row, first)
    if not starts:
        move.wait()
    per_dot = COLS // LANES
    high = 2 * COLS

    def multiply(n, carry):
        for cut in range(2 * slots // high):
            spec = lax.dot_general(
                table[cut * high : (cut + 1) * high, :],
                filt[pl.ds(pl.multiple_of(n * COLS, COLS), COLS), :],
                (((1,), (1,)), ((), ())),
                preferred_element_type=jnp.float32,
            )
            for h in range(per_dot):
                b = n * per_dot + h
                turn[pl.ds(pl.multiple_of(b * 2 * slots + cut * high, high), high), :] = (
                    spec[:, h * LANES : (h + 1) * LANES] * weight[pl.ds(b, 1), :]
                )
        return carry

    lax.fori_loop(0, pairs // per_dot, multiply, 0)

    def corner(out_ref, slot, at):
        real = turn[pl.ds(slot, pairs, stride=2 * slots), :]
        imag = turn[pl.ds(slots + slot, pairs, stride=2 * slots), :]
        out_ref[at] = jnp.concatenate([real, imag], axis=0).astype(jnp.bfloat16)

    def corners(out_ref, begin, at, count):
        def some(j, carry):
            for u in range(8):
                corner(out_ref, begin + j * 8 + u, at + j * 8 + u)
            return carry

        lax.fori_loop(0, count // 8, some, 0)

    if owners:
        own = out_refs[0].shape[0] // (owners // BLOCKS)
        for way in range(owners // BLOCKS):
            for other in range(BLOCKS):
                target = lax.rem(block + other, BLOCKS)
                begin = ((way // cores * BLOCKS + target) * cores + way % cores) * own
                corners(out_refs[other], begin, way * own, own)
    else:
        corners(out_refs[0], 0, 0, slots)
    if starts:
        move.wait()


def transform(place, spec_good, flags, voltages, coefs, table, after, row_first, rows, nexts=False, owners=0, cores=0):
    ins = flags.shape[0]
    taps, frame_len = coefs.shape
    starts = table.shape[1] == 1
    slots = table.shape[0] if starts else table.shape[0] // 2
    pairs = rows * ins // LANES
    flops = 2 * rows * ins * frame_len * 2 * slots
    smem = pl.BlockSpec(memory_space=pltpu.SMEM)
    vmem = pl.BlockSpec(memory_space=pltpu.VMEM)
    hbm = pl.BlockSpec(memory_space=pl.ANY)
    out_shape, out_specs = [], []
    if starts:
        out_shape.append(jax.ShapeDtypeStruct((2 * slots, frame_len), jnp.bfloat16))
        out_specs.append(hbm)
    if owners:
        out_shape += [jax.ShapeDtypeStruct((slots // BLOCKS, 2 * pairs, LANES), jnp.bfloat16)] * BLOCKS
    else:
        out_shape.append(jax.ShapeDtypeStruct((slots, 2 * pairs, LANES), jnp.bfloat16))
    out_specs += [vmem] * (len(out_shape) - len(out_specs))
    return pl.pallas_call(
        functools.partial(transform_kernel, row_first, rows, nexts, starts, owners, cores),
        out_shape=out_shape,
        in_specs=[smem, smem, vmem, hbm, vmem, vmem if starts else hbm, hbm],
        out_specs=out_specs,
        scratch_shapes=[
            pltpu.SMEM((rows,), jnp.int32),
            pltpu.VMEM((AHEAD, ins, frame_len), jnp.bfloat16),
            pltpu.VMEM((taps, frame_len // LANES, ins, LANES), jnp.float32),
            pltpu.VMEM((rows, flags.shape[1]), jnp.float32),
            pltpu.VMEM((pairs, LANES), jnp.float32),
            pltpu.VMEM((rows * ins, frame_len), jnp.bfloat16),
            pltpu.VMEM((pairs * 2 * slots, LANES), jnp.float32),
            pltpu.VMEM((2 * slots, frame_len), jnp.bfloat16),
            pltpu.SemaphoreType.DMA((AHEAD,)),
            pltpu.SemaphoreType.DMA,
        ],
        compiler_params=pltpu.CompilerParams(vmem_limit_bytes=VMEM_BYTES),
        cost_estimate=pl.CostEstimate(flops=8 * flops, bytes_accessed=12 * 2**20, transcendentals=0),
        name="filter_transform",
    )(place, spec_good, flags, voltages, coefs, table, voltages if after is None else after)


def correlate_kernel(chips, cores, pieces, *refs):
    scale_ref, refs = refs[0], refs[1:]
    part_refs = refs[:pieces]
    out_ref, straight, turned = refs[-3:]
    ins = LANES // cores
    total = straight.shape[1]
    half = total // 2
    scale = scale_ref[0]
    upper = lax.broadcasted_iota(jnp.int32, (half, half), 1) >= lax.broadcasted_iota(jnp.int32, (half, half), 0)

    def one_slot(slot, carry):
        for chip in range(chips):
            lanes = pl.ds(chip * LANES, LANES)
            place = 0
            for part in part_refs:
                columns = part.shape[0] // (chips * cores)
                depth = part.shape[2]
                half_depth = depth // 2
                low = lax.broadcasted_iota(jnp.int32, (depth, LANES), 1) < ins
                for column in range(columns):
                    sources = [(chip * columns + column) * cores + core for core in range(cores)]
                    one, two = (part[source, slot].astype(jnp.float32) for source in sources)
                    first = jnp.where(low, one, pltpu.roll(two, ins, 1))
                    second = jnp.where(low, pltpu.roll(one, ins, 1), two)
                    for both in (first, second):
                        rows = pl.ds(place, depth)
                        straight[rows, lanes] = both.astype(jnp.bfloat16)
                        turned[rows, lanes] = jnp.concatenate([-both[half_depth:], both[:half_depth]], axis=0).astype(jnp.bfloat16)
                        place += depth
        left = straight[...].T

        def product(a, ref, b):
            return jnp.dot(left[a * half : (a + 1) * half], ref[:, b * half : (b + 1) * half], preferred_element_type=jnp.float32) * scale

        for a in range(2):
            here = pl.ds(a * half, half)
            both = jnp.where(upper, product(a, straight, a), product(a, turned, a))
            out_ref[slot, here, here] = both.astype(out_ref.dtype)
        out_ref[slot, :half, half:] = product(0, straight, 1).astype(out_ref.dtype)
        out_ref[slot, half:, :half] = product(1, turned, 0).astype(out_ref.dtype)
        return carry

    lax.fori_loop(0, out_ref.shape[0], one_slot, 0, unroll=2)


def correlate(scale, parts, into, first, own, chips, cores):
    count = min(part.shape[1] - begin for part, begin in parts)
    total = chips * LANES
    depth = sum(part.shape[0] // chips * part.shape[2] for part, _ in parts)

    def spec(part, begin):
        return pl.BlockSpec((part.shape[0], SLOTS) + part.shape[2:], lambda c: (0, c + begin // SLOTS, 0, 0))

    arrays = [part for part, _ in parts]
    in_specs = [pl.BlockSpec(memory_space=pltpu.SMEM)] + [spec(*pair) for pair in parts]
    operands = [scale] + arrays
    aliases = {}
    kernel = functools.partial(correlate_kernel, chips, cores, len(parts))
    if into is not None:
        aliases = {len(operands): 0}
        operands.append(into)
        in_specs.append(pl.BlockSpec(memory_space=pl.ANY))
    return pl.pallas_call(
        kernel,
        grid=(count // SLOTS,),
        out_shape=jax.ShapeDtypeStruct((own, total, total), jnp.bfloat16),
        in_specs=in_specs,
        out_specs=pl.BlockSpec((SLOTS, total, total), lambda c: (c + first // SLOTS, 0, 0)),
        scratch_shapes=[pltpu.VMEM((depth, total), jnp.bfloat16)] * 2,
        input_output_aliases=aliases,
        compiler_params=pltpu.CompilerParams(vmem_limit_bytes=VMEM_BYTES),
        cost_estimate=pl.CostEstimate(
            flops=count * 8 * total * total * depth, bytes_accessed=count * 3 * total * total, transcendentals=0
        ),
        name="correlate",
    )(*operands)


def make_plain_table(channels, frame_len):
    samples = jnp.arange(frame_len, dtype=jnp.int32)
    phase_index = samples[:, None] * channels[None, :] % frame_len
    angles = phase_index.astype(jnp.float32) * (2.0 * math.pi / frame_len)
    norm_scale = 1.0 / math.sqrt(frame_len)
    return jnp.stack([jnp.cos(angles) * norm_scale, -jnp.sin(angles) * norm_scale], axis=1).astype(
        jnp.bfloat16
    )


def correlate_one(spectra_block):
    input_total = spectra_block.shape[0]
    half_width = spectra_block.shape[1] // 2
    rotated = jnp.concatenate(
        [spectra_block[:, half_width:], -spectra_block[:, :half_width]], axis=1
    )
    stacked = jnp.concatenate([spectra_block, rotated], axis=0)
    products = jnp.dot(stacked, spectra_block.T, preferred_element_type=jnp.float32)
    upper_mask = jnp.arange(input_total)[None, :] >= jnp.arange(input_total)[:, None]
    return jnp.where(upper_mask, products[:input_total], products[input_total:])


def rounded(values):
    return lax.optimization_barrier(values.astype(jnp.bfloat16)).astype(jnp.float32)


def local_plain(voltages, pfb_coeffs, input_flags, spec_good, chan_map):
    tap_count, frame_len = pfb_coeffs.shape
    local_inputs, block_len = input_flags.shape
    frames = voltages.reshape(local_inputs, block_len, frame_len)
    earlier = passed_along(frames[:, block_len - tap_count + 1 :, :], "tblk", 1)
    extended = jnp.concatenate([earlier, frames], axis=1)
    summed = jnp.zeros((local_inputs, block_len, frame_len), jnp.float32)
    for tap_index in range(tap_count):
        window_part = extended[:, tap_index : tap_index + block_len, :]
        summed = summed + pfb_coeffs[tap_index][None, None, :] * window_part.astype(jnp.float32)
    block_index = lax.axis_index("tblk")
    good_here = lax.dynamic_slice_in_dim(spec_good, block_index * block_len, block_len)
    weights = input_flags * good_here[None, :]
    filtered = (summed * weights.astype(jnp.float32)[:, :, None]).astype(jnp.bfloat16)
    inp_count = lax.axis_size("inp")
    tblk_count = lax.axis_size("tblk")
    sub_count = lax.axis_size("sub")
    chan_total = chan_map.shape[0]
    per_owner = chan_total // (inp_count * tblk_count * sub_count)
    live_total = jnp.sum(spec_good).astype(jnp.float32)
    slot_order = jnp.arange(chan_total).reshape(inp_count, tblk_count, sub_count, per_owner)
    slot_order = slot_order.transpose(0, 2, 1, 3).reshape(chan_total)
    dft_table = make_plain_table(chan_map[slot_order], frame_len)
    spectra = jnp.einsum("isn,nqj->jiqs", filtered, dft_table, preferred_element_type=jnp.float32)
    spectra = spectra.astype(jnp.bfloat16).reshape(chan_total, local_inputs, -1)
    turned = lax.all_to_all(spectra, ("inp", "sub"), split_axis=0, concat_axis=1, tiled=True)
    summed_vis = lax.psum_scatter(
        rounded(lax.map(correlate_one, turned)).astype(jnp.bfloat16),
        "tblk",
        scatter_dimension=0,
        tiled=True,
    ).astype(jnp.float32)
    return (summed_vis / live_total).astype(jnp.bfloat16)


def local(voltages, pfb_coeffs, input_flags, spec_good, chan_map):
    taps, frame_len = pfb_coeffs.shape
    ins, block_len = input_flags.shape
    chips, blocks, cores = (lax.axis_size(axis) for axis in ("inp", "tblk", "sub"))
    owners = chips * blocks * cores
    slots = chan_map.shape[0]
    own = slots // owners
    if blocks != BLOCKS or ins * cores != LANES or own % 16 or ins % 16 or slots % 64 or taps > STEP:
        return local_plain(voltages, pfb_coeffs, input_flags, spec_good, chan_map)
    ways = chips * cores
    block = lax.axis_index("tblk").astype(jnp.int32)
    scale = (1.0 / jnp.sum(spec_good).astype(jnp.float32)).reshape(1)
    next_flags = passed_along(input_flags[:, :taps], "tblk", -1)

    def chunk(row_first, rows, table, after, flags=input_flags, **rest):
        return transform(block.reshape(1), spec_good, flags, voltages, pfb_coeffs, table, after, row_first, rows, **rest)

    def swapped(piece):
        return lax.ppermute(piece, "tblk", [(0, 1), (1, 0)])

    def turn(piece, axes, before):
        if before is not None:
            piece, before = lax.optimization_barrier((piece, before))
        return lax.all_to_all(piece, axes, split_axis=0, concat_axis=0, tiled=True), before

    column = ("inp", "sub")
    table, early = chunk(STEP, STEP, chan_map.reshape(slots, 1), None)
    early = early.reshape(owners, own, *early.shape[1:])
    early, _ = turn(early, ("inp", "tblk", "sub"), None)
    split = dict(owners=owners, cores=cores)
    middle = [part.reshape(ways, own, *part.shape[1:]) for part in chunk(2 * STEP, 2 * STEP, table, table, **split)]
    middle_own, early = turn(middle[0], column, early)
    middle_other = swapped(middle[1])
    over = [part.reshape(ways, own, *part.shape[1:]) for part in chunk(0, STEP, table, middle[0], next_flags, nexts=True, **split)]
    late = [part.reshape(ways, own, *part.shape[1:]) for part in chunk(0, STEP, table, over[0], **split)]
    late_other, over_other = swapped(late[1]), swapped(over[1])
    middle_other, late[0] = lax.optimization_barrier((middle_other, late[0]))
    middle_other, middle_own = turn(middle_other, column, middle_own)

    def added(a, b, here):
        return (a.astype(jnp.float32) + jnp.where(here, b.astype(jnp.float32), 0.0)).astype(jnp.bfloat16)

    out, before = None, middle_other
    cut = own * 3 // 4
    tails = []
    for begin, end in ((0, cut), (cut, own)):
        mine = added(late[0][:, begin:end], over_other[:, begin:end], block > 0)
        others = added(late_other[:, begin:end], over[0][:, begin:end], block == 0)
        half = mine.shape[2] // 2
        piece = jnp.concatenate([mine[:, :, :half], others[:, :, :half], mine[:, :, half:], others[:, :, half:]], axis=2)
        tail, before = turn(piece, column, before)
        if tails:
            tails[0] = before
        else:
            middle_other = before
        tails.append(tail)
        before = tail
    for (begin, end), tail in zip(((0, cut), (cut, own)), tails):
        parts = [(early, begin), (middle_own, begin), (middle_other, begin), (tail, 0)]
        out = correlate(scale, parts, out, begin, own, chips, cores)
    return out


def solution(mesh):
    return jax.shard_map(
        local,
        mesh=mesh,
        in_specs=(
            P(("grp", "inp", "sub"), "tblk"),
            P(),
            P(("grp", "inp", "sub"), "tblk"),
            P("grp"),
            P(),
        ),
        out_specs=P(("grp", "inp", "tblk", "sub"), None, None),
        check_vma=False,
    )
```

```python
import functools
import math

import jax
import jax.numpy as jnp
from jax import lax
from jax.experimental import pallas as pl
from jax.experimental.pallas import tpu as pltpu
from jax.sharding import PartitionSpec as P

MAX_KEPT = 64
STEP = 16
LANES = 128
COLS = 256
PAD = 8
SLOTS = 4
BLOCKS = 2
AHEAD = 16
VMEM_BYTES = 56 * 1024 * 1024


def passed_along(value, axis, steps):
    count = lax.axis_size(axis)
    initial, last = (max(0, -steps), min(count, count - steps))
    return lax.ppermute(value, axis, [(source, source + steps) for source in range(initial, last)])


def turn_of(places, frame_len):
    quarter = frame_len // 4
    turns = (places + quarter // 2) // quarter
    angle = (places - turns * quarter).astype(jnp.float32) * (2.0 * math.pi / frame_len)
    square = angle * angle
    sine = angle * (1.0 + square * (-1.0 / 6 + square * (1.0 / 120 + square * (-1.0 / 5040 + square * (1.0 / 362880)))))
    cosine = 1.0 + square * (-0.5 + square * (1.0 / 24 + square * (-1.0 / 720 + square * (1.0 / 40320))))
    odd = (turns == 1) | (turns == 3)
    first, second = jnp.where(odd, sine, cosine), jnp.where(odd, cosine, sine)
    return (
        jnp.where((turns == 1) | (turns == 2), -first, first),
        jnp.where((turns == 2) | (turns == 3), -second, second),
    )


def fill_table(chan_ref, table_ref, frame_len):
    slots = chan_ref.shape[0]
    norm_scale = 1.0 / math.sqrt(frame_len)

    def block(step, carry):
        rows = pl.ds(pl.multiple_of(step * 64, 64), 64)
        lane = lax.broadcasted_iota(jnp.int32, (64, LANES), 1)
        channels = chan_ref[rows, :]
        fine_cos, fine_sin = turn_of(lax.rem(channels * lane, frame_len), frame_len)
        coarse_cos, coarse_sin = turn_of(lax.rem(channels * lane * LANES, frame_len), frame_len)
        coarse_cos, coarse_sin = coarse_cos * norm_scale, coarse_sin * norm_scale
        for part in range(frame_len // LANES):
            span = pl.ds(part * LANES, LANES)
            cosine, sine = coarse_cos[:, part : part + 1], coarse_sin[:, part : part + 1]
            below = pl.ds(pl.multiple_of(slots + step * 64, 64), 64)
            table_ref[rows, span] = (cosine * fine_cos - sine * fine_sin).astype(table_ref.dtype)
            table_ref[below, span] = -(sine * fine_cos + cosine * fine_sin).astype(table_ref.dtype)
        return carry

    lax.fori_loop(0, slots // 64, block, 0)


def transform_kernel(row_first, rows, nexts, starts, owners, cores, *refs):
    place_ref, good_ref, flag_ref, volt_ref, coef_ref, table_in, _, *refs = refs
    if starts:
        table_out, *refs = refs
    out_refs = refs[: BLOCKS if owners else 1]
    index_ref, raw, wide, hot, weight, filt, turn, table, sems, table_sem = refs[len(out_refs) :]
    taps, frame_len = coef_ref.shape
    ins = flag_ref.shape[0]
    blocks = BLOCKS
    block_len = good_ref.shape[0] // BLOCKS
    slots = table.shape[0] // 2
    ring, ahead = wide.shape[0], raw.shape[0]
    pairs = rows * ins // LANES
    stride = turn.shape[0] // pairs
    block = place_ref[0]

    if starts:
        move = pltpu.make_async_copy(table, table_out, table_sem)
    else:
        move = pltpu.make_async_copy(table_in, table, table_sem)
        move.start()

    def note(s, carry):
        seen, latest = carry
        if nexts:
            keep = (block + 1 < blocks) & (good_ref[jnp.minimum(block + 1, blocks - 1) * block_len + s] > 0)
        else:
            keep = good_ref[block * block_len + s] > 0
        mine = keep & (seen >= row_first) & (seen < row_first + rows)
        spectrum = s + block_len if nexts else s

        @pl.when(mine)
        def _():
            index_ref[seen - row_first] = spectrum

        return seen + keep.astype(jnp.int32), jnp.where(mine, spectrum, latest)

    span = taps - 1 if nexts else block_len
    seen, latest = lax.fori_loop(0, span, note, (jnp.int32(0), jnp.int32(block_len - 1)))
    used = jnp.clip(seen - row_first, 0, rows)

    def rest(r, carry):
        index_ref[r] = latest
        return carry

    lax.fori_loop(used, rows, rest, 0)
    first = index_ref[0]
    end = index_ref[rows - 1] + taps

    def inside(extended):
        return (extended >= taps - 1) & (extended < taps - 1 + block_len)

    def on_copy(extended):
        slot = lax.rem(extended, ahead)
        begin = pl.multiple_of((extended - (taps - 1)) * frame_len, frame_len)
        return pltpu.make_async_copy(volt_ref.at[:, pl.ds(begin, frame_len)], raw.at[slot], sems.at[slot])

    def fetch(extended):
        @pl.when((extended < end) & inside(extended))
        def _():
            on_copy(extended).start()

    for k in range(ahead):
        fetch(first + k)
    if starts:
        fill_table(table_in, table, frame_len)
        move.start()

    spectrum = lax.broadcasted_iota(jnp.int32, (1, hot.shape[1]), 1) + (block_len if nexts else 0)
    for r in range(rows):
        chosen = (spectrum == index_ref[r]) & (jnp.int32(r) < used)
        hot[pl.ds((r % 2) * (rows // 2) + r // 2, 1), :] = chosen.astype(jnp.float32)
    flags = flag_ref[...].astype(jnp.float32)
    weights = lax.dot_general(hot[...], flags, (((1,), (1,)), ((), ())), preferred_element_type=jnp.float32)
    weight[...] = jnp.concatenate([weights[: rows // 2], weights[rows // 2 :]], axis=1)

    def take(extended, carry):
        to, came = lax.rem(extended, ring), lax.rem(extended, ahead)

        @pl.when(inside(extended))
        def _():
            on_copy(extended).wait()
            for col in range(frame_len // LANES):
                wide[to, col] = raw[came, :, col * LANES : (col + 1) * LANES].astype(jnp.float32)

        @pl.when(jnp.logical_not(inside(extended)))
        def _():
            wide[to] = jnp.zeros(wide.shape[1:], wide.dtype)

        fetch(extended + ahead)
        return carry

    def filter_row(r, have):
        base = index_ref[r]
        lax.fori_loop(have, base + taps, take, 0)
        places = [lax.rem(base + k, ring) for k in range(taps)]
        at = pl.ds(pl.multiple_of(r * ins, ins), ins)

        def add_up(begin, stop):
            for col in range(frame_len // LANES):
                here = pl.ds(col * LANES, LANES)
                total = None
                for k in range(begin, stop):
                    term = wide[places[k], col] * coef_ref[pl.ds(k, 1), here]
                    total = term if total is None else total + term
                filt[at, here] = total.astype(jnp.bfloat16)

        half = taps // 2
        live = r < used
        early = (base + half <= taps - 1) if row_first == 0 and not nexts else False
        late = (base + half >= taps - 1 + block_len) if nexts else False

        @pl.when(live & jnp.logical_not(early | late))
        def _():
            add_up(0, taps)

        if row_first == 0 and not nexts:
            pl.when(live & early)(lambda: add_up(half, taps))
        if nexts:
            pl.when(live & late)(lambda: add_up(0, half))

        @pl.when(jnp.logical_not(live))
        def _():
            filt[at, :] = jnp.zeros((ins, frame_len), filt.dtype)

        return jnp.maximum(have, base + taps)

    lax.fori_loop(0, rows, filter_row, first)
    if not starts:
        move.wait()
    per_dot = COLS // LANES
    high = 2 * COLS

    def multiply(n, carry):
        for cut in range(2 * slots // high):
            spec = lax.dot_general(
                table[cut * high : (cut + 1) * high, :],
                filt[pl.ds(pl.multiple_of(n * COLS, COLS), COLS), :],
                (((1,), (1,)), ((), ())),
                preferred_element_type=jnp.float32,
            )
            for h in range(per_dot):
                b = n * per_dot + h
                turn[pl.ds(pl.multiple_of(b * stride + cut * high, 8), high), :] = (
                    spec[:, h * LANES : (h + 1) * LANES] * weight[pl.ds(b, 1), :]
                )
        return carry

    lax.fori_loop(0, pairs // per_dot, multiply, 0)

    def corner(out_ref, slot, at):
        real = turn[pl.ds(slot, pairs, stride=stride), :]
        imag = turn[pl.ds(slots + slot, pairs, stride=stride), :]
        out_ref[at] = jnp.concatenate([real, imag], axis=0).astype(jnp.bfloat16)

    def corners(out_ref, begin, at, count):
        def some(j, carry):
            for u in range(8):
                corner(out_ref, begin + j * 8 + u, at + j * 8 + u)
            return carry

        lax.fori_loop(0, count // 8, some, 0)

    if owners:
        own = out_refs[0].shape[0] // (owners // BLOCKS)
        for way in range(owners // BLOCKS):
            for other in range(BLOCKS):
                target = lax.rem(block + other, BLOCKS)
                begin = ((way // cores * BLOCKS + target) * cores + way % cores) * own
                corners(out_refs[other], begin, way * own, own)
    else:
        corners(out_refs[0], 0, 0, slots)
    if starts:
        move.wait()


def transform(place, spec_good, flags, voltages, coefs, table, after, row_first, rows, nexts=False, owners=0, cores=0):
    ins = flags.shape[0]
    taps, frame_len = coefs.shape
    starts = table.shape[1] == 1
    slots = table.shape[0] if starts else table.shape[0] // 2
    pairs = rows * ins // LANES
    flops = 2 * rows * ins * frame_len * 2 * slots
    smem = pl.BlockSpec(memory_space=pltpu.SMEM)
    vmem = pl.BlockSpec(memory_space=pltpu.VMEM)
    hbm = pl.BlockSpec(memory_space=pl.ANY)
    out_shape, out_specs = [], []
    if starts:
        out_shape.append(jax.ShapeDtypeStruct((2 * slots, frame_len), jnp.bfloat16))
        out_specs.append(hbm)
    if owners:
        out_shape += [jax.ShapeDtypeStruct((slots // BLOCKS, 2 * pairs, LANES), jnp.bfloat16)] * BLOCKS
    else:
        out_shape.append(jax.ShapeDtypeStruct((slots, 2 * pairs, LANES), jnp.bfloat16))
    out_specs += [vmem] * (len(out_shape) - len(out_specs))
    return pl.pallas_call(
        functools.partial(transform_kernel, row_first, rows, nexts, starts, owners, cores),
        out_shape=out_shape,
        in_specs=[smem, smem, vmem, hbm, vmem, vmem if starts else hbm, hbm],
        out_specs=out_specs,
        scratch_shapes=[
            pltpu.SMEM((rows,), jnp.int32),
            pltpu.VMEM((AHEAD, ins, frame_len), jnp.bfloat16),
            pltpu.VMEM((taps, frame_len // LANES, ins, LANES), jnp.float32),
            pltpu.VMEM((rows, flags.shape[1]), jnp.float32),
            pltpu.VMEM((pairs, LANES), jnp.float32),
            pltpu.VMEM((rows * ins, frame_len), jnp.bfloat16),
            pltpu.VMEM((pairs * (2 * slots + PAD), LANES), jnp.float32),
            pltpu.VMEM((2 * slots, frame_len), jnp.bfloat16),
            pltpu.SemaphoreType.DMA((AHEAD,)),
            pltpu.SemaphoreType.DMA,
        ],
        compiler_params=pltpu.CompilerParams(vmem_limit_bytes=VMEM_BYTES),
        cost_estimate=pl.CostEstimate(flops=8 * flops, bytes_accessed=12 * 2**20, transcendentals=0),
        name="filter_transform",
    )(place, spec_good, flags, voltages, coefs, table, voltages if after is None else after)


def correlate_kernel(chips, cores, pieces, *refs):
    scale_ref, refs = refs[0], refs[1:]
    part_refs = refs[:pieces]
    out_ref, straight, turned = refs[-3:]
    ins = LANES // cores
    total = straight.shape[1]
    half = total // 2
    scale = scale_ref[0]
    upper = lax.broadcasted_iota(jnp.int32, (half, half), 1) >= lax.broadcasted_iota(jnp.int32, (half, half), 0)

    def one_slot(slot, carry):
        for chip in range(chips):
            lanes = pl.ds(chip * LANES, LANES)
            place = 0
            for part in part_refs:
                columns = part.shape[0] // (chips * cores)
                depth = part.shape[2]
                half_depth = depth // 2
                low = lax.broadcasted_iota(jnp.int32, (depth, LANES), 1) < ins
                for column in range(columns):
                    sources = [(chip * columns + column) * cores + core for core in range(cores)]
                    one, two = (part[source, slot].astype(jnp.float32) for source in sources)
                    first = jnp.where(low, one, pltpu.roll(two, ins, 1))
                    second = jnp.where(low, pltpu.roll(one, ins, 1), two)
                    for both in (first, second):
                        rows = pl.ds(place, depth)
                        straight[rows, lanes] = both.astype(jnp.bfloat16)
                        turned[rows, lanes] = jnp.concatenate([-both[half_depth:], both[:half_depth]], axis=0).astype(jnp.bfloat16)
                        place += depth
        left = straight[...].T

        def product(a, ref, b):
            return jnp.dot(left[a * half : (a + 1) * half], ref[:, b * half : (b + 1) * half], preferred_element_type=jnp.float32) * scale

        for a in range(2):
            here = pl.ds(a * half, half)
            both = jnp.where(upper, product(a, straight, a), product(a, turned, a))
            out_ref[slot, here, here] = both.astype(out_ref.dtype)
        out_ref[slot, :half, half:] = product(0, straight, 1).astype(out_ref.dtype)
        out_ref[slot, half:, :half] = product(1, turned, 0).astype(out_ref.dtype)
        return carry

    lax.fori_loop(0, out_ref.shape[0], one_slot, 0, unroll=2)


def correlate(scale, parts, into, first, own, chips, cores):
    count = min(part.shape[1] - begin for part, begin in parts)
    total = chips * LANES
    depth = sum(part.shape[0] // chips * part.shape[2] for part, _ in parts)

    def spec(part, begin):
        return pl.BlockSpec((part.shape[0], SLOTS) + part.shape[2:], lambda c: (0, c + begin // SLOTS, 0, 0))

    arrays = [part for part, _ in parts]
    in_specs = [pl.BlockSpec(memory_space=pltpu.SMEM)] + [spec(*pair) for pair in parts]
    operands = [scale] + arrays
    aliases = {}
    kernel = functools.partial(correlate_kernel, chips, cores, len(parts))
    if into is not None:
        aliases = {len(operands): 0}
        operands.append(into)
        in_specs.append(pl.BlockSpec(memory_space=pl.ANY))
    return pl.pallas_call(
        kernel,
        grid=(count // SLOTS,),
        out_shape=jax.ShapeDtypeStruct((own, total, total), jnp.bfloat16),
        in_specs=in_specs,
        out_specs=pl.BlockSpec((SLOTS, total, total), lambda c: (c + first // SLOTS, 0, 0)),
        scratch_shapes=[pltpu.VMEM((depth, total), jnp.bfloat16)] * 2,
        input_output_aliases=aliases,
        compiler_params=pltpu.CompilerParams(vmem_limit_bytes=VMEM_BYTES),
        cost_estimate=pl.CostEstimate(
            flops=count * 8 * total * total * depth, bytes_accessed=count * 3 * total * total, transcendentals=0
        ),
        name="correlate",
    )(*operands)


def make_plain_table(channels, frame_len):
    samples = jnp.arange(frame_len, dtype=jnp.int32)
    phase_index = samples[:, None] * channels[None, :] % frame_len
    angles = phase_index.astype(jnp.float32) * (2.0 * math.pi / frame_len)
    norm_scale = 1.0 / math.sqrt(frame_len)
    return jnp.stack([jnp.cos(angles) * norm_scale, -jnp.sin(angles) * norm_scale], axis=1).astype(
        jnp.bfloat16
    )


def correlate_one(spectra_block):
    input_total = spectra_block.shape[0]
    half_width = spectra_block.shape[1] // 2
    rotated = jnp.concatenate(
        [spectra_block[:, half_width:], -spectra_block[:, :half_width]], axis=1
    )
    stacked = jnp.concatenate([spectra_block, rotated], axis=0)
    products = jnp.dot(stacked, spectra_block.T, preferred_element_type=jnp.float32)
    upper_mask = jnp.arange(input_total)[None, :] >= jnp.arange(input_total)[:, None]
    return jnp.where(upper_mask, products[:input_total], products[input_total:])


def rounded(values):
    return lax.optimization_barrier(values.astype(jnp.bfloat16)).astype(jnp.float32)


def local_plain(voltages, pfb_coeffs, input_flags, spec_good, chan_map):
    tap_count, frame_len = pfb_coeffs.shape
    local_inputs, block_len = input_flags.shape
    frames = voltages.reshape(local_inputs, block_len, frame_len)
    earlier = passed_along(frames[:, block_len - tap_count + 1 :, :], "tblk", 1)
    extended = jnp.concatenate([earlier, frames], axis=1)
    summed = jnp.zeros((local_inputs, block_len, frame_len), jnp.float32)
    for tap_index in range(tap_count):
        window_part = extended[:, tap_index : tap_index + block_len, :]
        summed = summed + pfb_coeffs[tap_index][None, None, :] * window_part.astype(jnp.float32)
    block_index = lax.axis_index("tblk")
    good_here = lax.dynamic_slice_in_dim(spec_good, block_index * block_len, block_len)
    weights = input_flags * good_here[None, :]
    filtered = (summed * weights.astype(jnp.float32)[:, :, None]).astype(jnp.bfloat16)
    inp_count = lax.axis_size("inp")
    tblk_count = lax.axis_size("tblk")
    sub_count = lax.axis_size("sub")
    chan_total = chan_map.shape[0]
    per_owner = chan_total // (inp_count * tblk_count * sub_count)
    live_total = jnp.sum(spec_good).astype(jnp.float32)
    slot_order = jnp.arange(chan_total).reshape(inp_count, tblk_count, sub_count, per_owner)
    slot_order = slot_order.transpose(0, 2, 1, 3).reshape(chan_total)
    dft_table = make_plain_table(chan_map[slot_order], frame_len)
    spectra = jnp.einsum("isn,nqj->jiqs", filtered, dft_table, preferred_element_type=jnp.float32)
    spectra = spectra.astype(jnp.bfloat16).reshape(chan_total, local_inputs, -1)
    turned = lax.all_to_all(spectra, ("inp", "sub"), split_axis=0, concat_axis=1, tiled=True)
    summed_vis = lax.psum_scatter(
        rounded(lax.map(correlate_one, turned)).astype(jnp.bfloat16),
        "tblk",
        scatter_dimension=0,
        tiled=True,
    ).astype(jnp.float32)
    return (summed_vis / live_total).astype(jnp.bfloat16)


def local(voltages, pfb_coeffs, input_flags, spec_good, chan_map):
    taps, frame_len = pfb_coeffs.shape
    ins, block_len = input_flags.shape
    chips, blocks, cores = (lax.axis_size(axis) for axis in ("inp", "tblk", "sub"))
    owners = chips * blocks * cores
    slots = chan_map.shape[0]
    own = slots // owners
    if blocks != BLOCKS or ins * cores != LANES or own % 16 or ins % 16 or slots % 64 or taps > STEP:
        return local_plain(voltages, pfb_coeffs, input_flags, spec_good, chan_map)
    ways = chips * cores
    block = lax.axis_index("tblk").astype(jnp.int32)
    scale = (1.0 / jnp.sum(spec_good).astype(jnp.float32)).reshape(1)
    next_flags = passed_along(input_flags[:, :taps], "tblk", -1)

    def chunk(row_first, rows, table, after, flags=input_flags, **rest):
        return transform(block.reshape(1), spec_good, flags, voltages, pfb_coeffs, table, after, row_first, rows, **rest)

    def swapped(piece):
        return lax.ppermute(piece, "tblk", [(0, 1), (1, 0)])

    def turn(piece, axes, before):
        if before is not None:
            piece, before = lax.optimization_barrier((piece, before))
        return lax.all_to_all(piece, axes, split_axis=0, concat_axis=0, tiled=True), before

    column = ("inp", "sub")
    table, early = chunk(STEP, STEP, chan_map.reshape(slots, 1), None)
    early = early.reshape(owners, own, *early.shape[1:])
    early, _ = turn(early, ("inp", "tblk", "sub"), None)
    split = dict(owners=owners, cores=cores)
    middle = [part.reshape(ways, own, *part.shape[1:]) for part in chunk(2 * STEP, 2 * STEP, table, table, **split)]
    middle_own, early = turn(middle[0], column, early)
    middle_other = swapped(middle[1])
    over = [part.reshape(ways, own, *part.shape[1:]) for part in chunk(0, STEP, table, middle[0], next_flags, nexts=True, **split)]
    late = [part.reshape(ways, own, *part.shape[1:]) for part in chunk(0, STEP, table, over[0], **split)]
    late_other, over_other = swapped(late[1]), swapped(over[1])
    middle_other, late[0] = lax.optimization_barrier((middle_other, late[0]))
    middle_other, middle_own = turn(middle_other, column, middle_own)

    def added(a, b, here):
        return (a.astype(jnp.float32) + jnp.where(here, b.astype(jnp.float32), 0.0)).astype(jnp.bfloat16)

    out, before = None, middle_other
    cut = own * 3 // 4
    tails = []
    for begin, end in ((0, cut), (cut, own)):
        mine = added(late[0][:, begin:end], over_other[:, begin:end], block > 0)
        others = added(late_other[:, begin:end], over[0][:, begin:end], block == 0)
        half = mine.shape[2] // 2
        piece = jnp.concatenate([mine[:, :, :half], others[:, :, :half], mine[:, :, half:], others[:, :, half:]], axis=2)
        tail, before = turn(piece, column, before)
        if tails:
            tails[0] = before
        else:
            middle_other = before
        tails.append(tail)
        before = tail
    for (begin, end), tail in zip(((0, cut), (cut, own)), tails):
        parts = [(early, begin), (middle_own, begin), (middle_other, begin), (tail, 0)]
        out = correlate(scale, parts, out, begin, own, chips, cores)
    return out


def solution(mesh):
    return jax.shard_map(
        local,
        mesh=mesh,
        in_specs=(
            P(("grp", "inp", "sub"), "tblk"),
            P(),
            P(("grp", "inp", "sub"), "tblk"),
            P("grp"),
            P(),
        ),
        out_specs=P(("grp", "inp", "tblk", "sub"), None, None),
        check_vma=False,
    )
```

```python
import functools
import math

import jax
import jax.numpy as jnp
from jax import lax
from jax.experimental import pallas as pl
from jax.experimental.pallas import tpu as pltpu
from jax.sharding import PartitionSpec as P

MAX_KEPT = 64
STEP = 16
LANES = 128
COLS = 256
PAD = 8
SLOTS = 4
BLOCKS = 2
AHEAD = 16
VMEM_BYTES = 56 * 1024 * 1024


def passed_along(value, axis, steps):
    count = lax.axis_size(axis)
    initial, last = (max(0, -steps), min(count, count - steps))
    return lax.ppermute(value, axis, [(source, source + steps) for source in range(initial, last)])


def turn_of(places, frame_len):
    quarter = frame_len // 4
    turns = (places + quarter // 2) // quarter
    angle = (places - turns * quarter).astype(jnp.float32) * (2.0 * math.pi / frame_len)
    square = angle * angle
    sine = angle * (1.0 + square * (-1.0 / 6 + square * (1.0 / 120 + square * (-1.0 / 5040 + square * (1.0 / 362880)))))
    cosine = 1.0 + square * (-0.5 + square * (1.0 / 24 + square * (-1.0 / 720 + square * (1.0 / 40320))))
    odd = (turns == 1) | (turns == 3)
    first, second = jnp.where(odd, sine, cosine), jnp.where(odd, cosine, sine)
    return (
        jnp.where((turns == 1) | (turns == 2), -first, first),
        jnp.where((turns == 2) | (turns == 3), -second, second),
    )


def fill_table(chan_ref, table_ref, frame_len):
    slots = chan_ref.shape[0]
    norm_scale = 1.0 / math.sqrt(frame_len)

    def block(step, carry):
        rows = pl.ds(pl.multiple_of(step * 64, 64), 64)
        lane = lax.broadcasted_iota(jnp.int32, (64, LANES), 1)
        channels = chan_ref[rows, :]
        fine_cos, fine_sin = turn_of(lax.rem(channels * lane, frame_len), frame_len)
        coarse_cos, coarse_sin = turn_of(lax.rem(channels * lane * LANES, frame_len), frame_len)
        coarse_cos, coarse_sin = coarse_cos * norm_scale, coarse_sin * norm_scale
        for part in range(frame_len // LANES):
            span = pl.ds(part * LANES, LANES)
            cosine, sine = coarse_cos[:, part : part + 1], coarse_sin[:, part : part + 1]
            below = pl.ds(pl.multiple_of(slots + step * 64, 64), 64)
            table_ref[rows, span] = (cosine * fine_cos - sine * fine_sin).astype(table_ref.dtype)
            table_ref[below, span] = -(sine * fine_cos + cosine * fine_sin).astype(table_ref.dtype)
        return carry

    lax.fori_loop(0, slots // 64, block, 0)


def transform_kernel(row_first, rows, nexts, starts, owners, cores, *refs):
    place_ref, good_ref, flag_ref, volt_ref, coef_ref, table_in, _, *refs = refs
    if starts:
        table_out, *refs = refs
    out_refs = refs[: BLOCKS if owners else 1]
    index_ref, raw, wide, hot, weight, filt, turn, table, sems, table_sem = refs[len(out_refs) :]
    taps, frame_len = coef_ref.shape
    ins = flag_ref.shape[0]
    blocks = BLOCKS
    block_len = good_ref.shape[0] // BLOCKS
    slots = table.shape[0] // 2
    ring, ahead = wide.shape[0], raw.shape[0]
    pairs = rows * ins // LANES
    stride = turn.shape[0] // pairs
    block = place_ref[0]

    if starts:
        move = pltpu.make_async_copy(table, table_out, table_sem)
    else:
        move = pltpu.make_async_copy(table_in, table, table_sem)
        move.start()

    def note(s, carry):
        seen, latest = carry
        if nexts:
            keep = (block + 1 < blocks) & (good_ref[jnp.minimum(block + 1, blocks - 1) * block_len + s] > 0)
        else:
            keep = good_ref[block * block_len + s] > 0
        mine = keep & (seen >= row_first) & (seen < row_first + rows)
        spectrum = s + block_len if nexts else s

        @pl.when(mine)
        def _():
            index_ref[seen - row_first] = spectrum

        return seen + keep.astype(jnp.int32), jnp.where(mine, spectrum, latest)

    span = taps - 1 if nexts else block_len
    seen, latest = lax.fori_loop(0, span, note, (jnp.int32(0), jnp.int32(block_len - 1)))
    used = jnp.clip(seen - row_first, 0, rows)

    def rest(r, carry):
        index_ref[r] = latest
        return carry

    lax.fori_loop(used, rows, rest, 0)
    first = index_ref[0]
    end = index_ref[rows - 1] + taps

    def inside(extended):
        return (extended >= taps - 1) & (extended < taps - 1 + block_len)

    def on_copy(extended):
        slot = lax.rem(extended, ahead)
        begin = pl.multiple_of((extended - (taps - 1)) * frame_len, frame_len)
        return pltpu.make_async_copy(volt_ref.at[:, pl.ds(begin, frame_len)], raw.at[slot], sems.at[slot])

    def fetch(extended):
        @pl.when((extended < end) & inside(extended))
        def _():
            on_copy(extended).start()

    for k in range(ahead):
        fetch(first + k)
    if starts:
        fill_table(table_in, table, frame_len)
        move.start()

    spectrum = lax.broadcasted_iota(jnp.int32, (1, hot.shape[1]), 1) + (block_len if nexts else 0)
    for r in range(rows):
        chosen = (spectrum == index_ref[r]) & (jnp.int32(r) < used)
        hot[pl.ds((r % 2) * (rows // 2) + r // 2, 1), :] = chosen.astype(jnp.float32)
    flags = flag_ref[...].astype(jnp.float32)
    weights = lax.dot_general(hot[...], flags, (((1,), (1,)), ((), ())), preferred_element_type=jnp.float32)
    weight[...] = jnp.concatenate([weights[: rows // 2], weights[rows // 2 :]], axis=1)

    def take(extended, carry):
        to, came = lax.rem(extended, ring), lax.rem(extended, ahead)

        @pl.when(inside(extended))
        def _():
            on_copy(extended).wait()
            for col in range(frame_len // LANES):
                wide[to, col] = raw[came, :, col * LANES : (col + 1) * LANES].astype(jnp.float32)

        @pl.when(jnp.logical_not(inside(extended)))
        def _():
            wide[to] = jnp.zeros(wide.shape[1:], wide.dtype)

        fetch(extended + ahead)
        return carry

    def filter_row(r, have):
        base = index_ref[r]
        lax.fori_loop(have, base + taps, take, 0)
        places = [lax.rem(base + k, ring) for k in range(taps)]
        at = pl.ds(pl.multiple_of(r * ins, ins), ins)

        def add_up(begin, stop):
            for col in range(frame_len // LANES):
                here = pl.ds(col * LANES, LANES)
                total = None
                for k in range(begin, stop):
                    term = wide[places[k], col] * coef_ref[pl.ds(k, 1), here]
                    total = term if total is None else total + term
                filt[at, here] = total.astype(jnp.bfloat16)

        half = taps // 2
        live = r < used
        early = (base + half <= taps - 1) if row_first == 0 and not nexts else False
        late = (base + half >= taps - 1 + block_len) if nexts else False

        @pl.when(live & jnp.logical_not(early | late))
        def _():
            add_up(0, taps)

        if row_first == 0 and not nexts:
            pl.when(live & early)(lambda: add_up(half, taps))
        if nexts:
            pl.when(live & late)(lambda: add_up(0, half))

        @pl.when(jnp.logical_not(live))
        def _():
            filt[at, :] = jnp.zeros((ins, frame_len), filt.dtype)

        return jnp.maximum(have, base + taps)

    lax.fori_loop(0, rows, filter_row, first)
    if not starts:
        move.wait()
    per_dot = COLS // LANES
    high = 2 * COLS

    def multiply(n, carry):
        for cut in range(2 * slots // high):
            spec = lax.dot_general(
                table[cut * high : (cut + 1) * high, :],
                filt[pl.ds(pl.multiple_of(n * COLS, COLS), COLS), :],
                (((1,), (1,)), ((), ())),
                preferred_element_type=jnp.float32,
            )
            for h in range(per_dot):
                b = n * per_dot + h
                turn[pl.ds(pl.multiple_of(b * stride + cut * high, 8), high), :] = (
                    spec[:, h * LANES : (h + 1) * LANES] * weight[pl.ds(b, 1), :]
                )
        return carry

    lax.fori_loop(0, pairs // per_dot, multiply, 0)

    def corner(out_ref, slot, at):
        real = turn[pl.ds(slot, pairs, stride=stride), :]
        imag = turn[pl.ds(slots + slot, pairs, stride=stride), :]
        out_ref[at] = jnp.concatenate([real, imag], axis=0).astype(jnp.bfloat16)

    def corners(out_ref, begin, at, count):
        def some(j, carry):
            for u in range(8):
                corner(out_ref, begin + j * 8 + u, at + j * 8 + u)
            return carry

        lax.fori_loop(0, count // 8, some, 0)

    if owners:
        ways = owners // BLOCKS
        own = out_refs[0].shape[0] // ways
        for way in range(ways):
            for other in range(BLOCKS):
                chip = lax.rem(place_ref[1 + 2 * other] + way // cores, ways // cores)
                core = lax.rem(place_ref[2 + 2 * other] + way % cores, cores)
                target = lax.rem(block + other, BLOCKS)
                begin = ((chip * BLOCKS + target) * cores + core) * own
                corners(out_refs[other], begin, way * own, own)
    else:
        corners(out_refs[0], 0, 0, slots)
    if starts:
        move.wait()


def transform(place, spec_good, flags, voltages, coefs, table, after, row_first, rows, nexts=False, owners=0, cores=0):
    ins = flags.shape[0]
    taps, frame_len = coefs.shape
    starts = table.shape[1] == 1
    slots = table.shape[0] if starts else table.shape[0] // 2
    pairs = rows * ins // LANES
    flops = 2 * rows * ins * frame_len * 2 * slots
    smem = pl.BlockSpec(memory_space=pltpu.SMEM)
    vmem = pl.BlockSpec(memory_space=pltpu.VMEM)
    hbm = pl.BlockSpec(memory_space=pl.ANY)
    out_shape, out_specs = [], []
    if starts:
        out_shape.append(jax.ShapeDtypeStruct((2 * slots, frame_len), jnp.bfloat16))
        out_specs.append(hbm)
    if owners:
        out_shape += [jax.ShapeDtypeStruct((slots // BLOCKS, 2 * pairs, LANES), jnp.bfloat16)] * BLOCKS
    else:
        out_shape.append(jax.ShapeDtypeStruct((slots, 2 * pairs, LANES), jnp.bfloat16))
    out_specs += [vmem] * (len(out_shape) - len(out_specs))
    return pl.pallas_call(
        functools.partial(transform_kernel, row_first, rows, nexts, starts, owners, cores),
        out_shape=out_shape,
        in_specs=[smem, smem, vmem, hbm, vmem, vmem if starts else hbm, hbm],
        out_specs=out_specs,
        scratch_shapes=[
            pltpu.SMEM((rows,), jnp.int32),
            pltpu.VMEM((AHEAD, ins, frame_len), jnp.bfloat16),
            pltpu.VMEM((taps, frame_len // LANES, ins, LANES), jnp.float32),
            pltpu.VMEM((rows, flags.shape[1]), jnp.float32),
            pltpu.VMEM((pairs, LANES), jnp.float32),
            pltpu.VMEM((rows * ins, frame_len), jnp.bfloat16),
            pltpu.VMEM((pairs * (2 * slots + PAD), LANES), jnp.float32),
            pltpu.VMEM((2 * slots, frame_len), jnp.bfloat16),
            pltpu.SemaphoreType.DMA((AHEAD,)),
            pltpu.SemaphoreType.DMA,
        ],
        compiler_params=pltpu.CompilerParams(vmem_limit_bytes=VMEM_BYTES),
        cost_estimate=pl.CostEstimate(flops=6 * flops, bytes_accessed=12 * 2**20, transcendentals=0),
        name="filter_transform",
    )(place, spec_good, flags, voltages, coefs, table, voltages if after is None else after)


def correlate_kernel(chips, cores, kinds, *refs):
    scale_ref, place_ref, *refs = refs
    part_refs = []
    for by_way in kinds:
        count = chips * cores if by_way else 1
        part_refs.append(refs[:count])
        refs = refs[count:]
    out_ref, straight, turned = refs[-3:]
    ins = LANES // cores
    total = straight.shape[1]
    half = total // 2
    scale = scale_ref[0]
    upper = lax.broadcasted_iota(jnp.int32, (half, half), 1) >= lax.broadcasted_iota(jnp.int32, (half, half), 0)

    def one_slot(slot, carry):
        place = 0
        for by_way, part in zip(kinds, part_refs):
            depth = part[0].shape[-2]
            half_depth = depth // 2
            low = lax.broadcasted_iota(jnp.int32, (depth, LANES), 1) < ins
            columns = 1 if by_way else part[0].shape[0] // (chips * cores)
            for column in range(columns):
                for step in range(chips):
                    if by_way:
                        chip = lax.rem(place_ref[0] + chips - step, chips)
                        same, cross = (part[step * cores + core][slot].astype(jnp.float32) for core in range(cores))
                        one = jnp.where(place_ref[1] == 0, same, cross)
                        two = jnp.where(place_ref[1] == 0, cross, same)
                    else:
                        chip = step
                        sources = [(chip * columns + column) * cores + core for core in range(cores)]
                        one, two = (part[0][source, slot].astype(jnp.float32) for source in sources)
                    lanes = pl.ds(pl.multiple_of(chip * LANES, LANES), LANES) if by_way else pl.ds(chip * LANES, LANES)
                    first = jnp.where(low, one, pltpu.roll(two, ins, 1))
                    second = jnp.where(low, pltpu.roll(one, ins, 1), two)
                    for index, both in enumerate((first, second)):
                        rows = pl.ds(place + index * depth, depth)
                        straight[rows, lanes] = both.astype(jnp.bfloat16)
                        turned[rows, lanes] = jnp.concatenate([-both[half_depth:], both[:half_depth]], axis=0).astype(jnp.bfloat16)
                place += 2 * depth
        left = straight[...].T

        def product(a, ref, b):
            return jnp.dot(left[a * half : (a + 1) * half], ref[:, b * half : (b + 1) * half], preferred_element_type=jnp.float32) * scale

        for a in range(2):
            here = pl.ds(a * half, half)
            both = jnp.where(upper, product(a, straight, a), product(a, turned, a))
            out_ref[slot, here, here] = both.astype(out_ref.dtype)
        out_ref[slot, :half, half:] = product(0, straight, 1).astype(out_ref.dtype)
        out_ref[slot, half:, :half] = product(1, turned, 0).astype(out_ref.dtype)
        return carry

    lax.fori_loop(0, out_ref.shape[0], one_slot, 0, unroll=2)


def correlate(scale, spot, parts, into, first, count, own, chips, cores):
    total = chips * LANES
    arrays, in_specs, kinds, depth = [], [], [], 0
    for part, begin in parts:
        kinds.append(isinstance(part, list))
        for array in part if kinds[-1] else [part]:
            lead = () if kinds[-1] else (array.shape[0],)
            tail = array.shape[-2:]
            arrays.append(array)
            at = begin // SLOTS
            if lead:
                in_specs.append(pl.BlockSpec(lead + (SLOTS,) + tail, lambda c, at=at: (0, c + at, 0, 0)))
            else:
                in_specs.append(pl.BlockSpec((SLOTS,) + tail, lambda c, at=at: (c + at, 0, 0)))
        depth += cores * array.shape[-2] * (1 if kinds[-1] else array.shape[0] // (chips * cores))
    smem = pl.BlockSpec(memory_space=pltpu.SMEM)
    in_specs = [smem, smem] + in_specs
    operands = [scale, spot] + arrays
    aliases = {}
    kernel = functools.partial(correlate_kernel, chips, cores, tuple(kinds))
    if into is not None:
        aliases = {len(operands): 0}
        operands.append(into)
        in_specs.append(pl.BlockSpec(memory_space=pl.ANY))
    return pl.pallas_call(
        kernel,
        grid=(count // SLOTS,),
        out_shape=jax.ShapeDtypeStruct((own, total, total), jnp.bfloat16),
        in_specs=in_specs,
        out_specs=pl.BlockSpec((SLOTS, total, total), lambda c: (c + first // SLOTS, 0, 0)),
        scratch_shapes=[pltpu.VMEM((depth, total), jnp.bfloat16)] * 2,
        input_output_aliases=aliases,
        compiler_params=pltpu.CompilerParams(vmem_limit_bytes=VMEM_BYTES),
        cost_estimate=pl.CostEstimate(
            flops=count * 8 * total * total * depth, bytes_accessed=count * 3 * total * total, transcendentals=0
        ),
        name="correlate",
    )(*operands)


def make_plain_table(channels, frame_len):
    samples = jnp.arange(frame_len, dtype=jnp.int32)
    phase_index = samples[:, None] * channels[None, :] % frame_len
    angles = phase_index.astype(jnp.float32) * (2.0 * math.pi / frame_len)
    norm_scale = 1.0 / math.sqrt(frame_len)
    return jnp.stack([jnp.cos(angles) * norm_scale, -jnp.sin(angles) * norm_scale], axis=1).astype(
        jnp.bfloat16
    )


def correlate_one(spectra_block):
    input_total = spectra_block.shape[0]
    half_width = spectra_block.shape[1] // 2
    rotated = jnp.concatenate(
        [spectra_block[:, half_width:], -spectra_block[:, :half_width]], axis=1
    )
    stacked = jnp.concatenate([spectra_block, rotated], axis=0)
    products = jnp.dot(stacked, spectra_block.T, preferred_element_type=jnp.float32)
    upper_mask = jnp.arange(input_total)[None, :] >= jnp.arange(input_total)[:, None]
    return jnp.where(upper_mask, products[:input_total], products[input_total:])


def rounded(values):
    return lax.optimization_barrier(values.astype(jnp.bfloat16)).astype(jnp.float32)


def local_plain(voltages, pfb_coeffs, input_flags, spec_good, chan_map):
    tap_count, frame_len = pfb_coeffs.shape
    local_inputs, block_len = input_flags.shape
    frames = voltages.reshape(local_inputs, block_len, frame_len)
    earlier = passed_along(frames[:, block_len - tap_count + 1 :, :], "tblk", 1)
    extended = jnp.concatenate([earlier, frames], axis=1)
    summed = jnp.zeros((local_inputs, block_len, frame_len), jnp.float32)
    for tap_index in range(tap_count):
        window_part = extended[:, tap_index : tap_index + block_len, :]
        summed = summed + pfb_coeffs[tap_index][None, None, :] * window_part.astype(jnp.float32)
    block_index = lax.axis_index("tblk")
    good_here = lax.dynamic_slice_in_dim(spec_good, block_index * block_len, block_len)
    weights = input_flags * good_here[None, :]
    filtered = (summed * weights.astype(jnp.float32)[:, :, None]).astype(jnp.bfloat16)
    inp_count = lax.axis_size("inp")
    tblk_count = lax.axis_size("tblk")
    sub_count = lax.axis_size("sub")
    chan_total = chan_map.shape[0]
    per_owner = chan_total // (inp_count * tblk_count * sub_count)
    live_total = jnp.sum(spec_good).astype(jnp.float32)
    slot_order = jnp.arange(chan_total).reshape(inp_count, tblk_count, sub_count, per_owner)
    slot_order = slot_order.transpose(0, 2, 1, 3).reshape(chan_total)
    dft_table = make_plain_table(chan_map[slot_order], frame_len)
    spectra = jnp.einsum("isn,nqj->jiqs", filtered, dft_table, preferred_element_type=jnp.float32)
    spectra = spectra.astype(jnp.bfloat16).reshape(chan_total, local_inputs, -1)
    turned = lax.all_to_all(spectra, ("inp", "sub"), split_axis=0, concat_axis=1, tiled=True)
    summed_vis = lax.psum_scatter(
        rounded(lax.map(correlate_one, turned)).astype(jnp.bfloat16),
        "tblk",
        scatter_dimension=0,
        tiled=True,
    ).astype(jnp.float32)
    return (summed_vis / live_total).astype(jnp.bfloat16)


def local(voltages, pfb_coeffs, input_flags, spec_good, chan_map):
    taps, frame_len = pfb_coeffs.shape
    ins, block_len = input_flags.shape
    chips, blocks, cores = (lax.axis_size(axis) for axis in ("inp", "tblk", "sub"))
    owners = chips * blocks * cores
    slots = chan_map.shape[0]
    own = slots // owners
    if blocks != BLOCKS or ins * cores != LANES or own % 16 or ins % 16 or slots % 64 or taps > STEP:
        return local_plain(voltages, pfb_coeffs, input_flags, spec_good, chan_map)
    ways = chips * cores
    block = lax.axis_index("tblk").astype(jnp.int32)
    scale = (1.0 / jnp.sum(spec_good).astype(jnp.float32)).reshape(1)
    next_flags = passed_along(input_flags[:, :taps], "tblk", -1)

    spot = jnp.stack([lax.axis_index("inp"), lax.axis_index("sub")]).astype(jnp.int32)
    start = jnp.zeros((2,), jnp.int32)

    def chunk(row_first, rows, table, after, flags=input_flags, begin=(start, start), **rest):
        place = jnp.concatenate([block.reshape(1), *begin])
        return transform(place, spec_good, flags, voltages, pfb_coeffs, table, after, row_first, rows, **rest)

    def swapped(piece):
        return lax.ppermute(piece, "tblk", [(0, 1), (1, 0)])

    def turn(piece, axes, before):
        if before is not None:
            piece, before = lax.optimization_barrier((piece, before))
        return lax.all_to_all(piece, axes, split_axis=0, concat_axis=0, tiled=True), before

    column = ("inp", "sub")

    def sent(way, piece):
        if way == 0:
            return piece
        step, other = way // cores, way % cores
        pairs = [
            (chip * cores + core, (chip + step) % chips * cores + (core + other) % cores)
            for chip in range(chips)
            for core in range(cores)
        ]
        return lax.ppermute(piece, column, pairs)

    order = sorted(range(ways), key=lambda way: (-min(way // cores, chips - way // cores), way))

    def spread(pieces):
        came = {way: sent(way, pieces(way)) for way in order}
        return [came[way] for way in range(ways)]

    table, early = chunk(STEP, STEP, chan_map.reshape(slots, 1), None)
    early = early.reshape(owners, own, *early.shape[1:])
    early, _ = turn(early, ("inp", "tblk", "sub"), None)
    split = dict(owners=owners, cores=cores)
    middle = [part.reshape(ways, own, *part.shape[1:]) for part in chunk(2 * STEP, 2 * STEP, table, table, begin=(start, start), **split)]
    middle_own, early = turn(middle[0], column, early)
    middle_other = swapped(middle[1])
    over = [part.reshape(ways, own, *part.shape[1:]) for part in chunk(0, STEP, table, middle[0], next_flags, begin=(spot, spot), nexts=True, **split)]
    late = [part.reshape(ways, own, *part.shape[1:]) for part in chunk(0, STEP, table, over[0], begin=(spot, spot), **split)]
    groups = [(0, own // 2), (own // 2, own)]
    whole = [swapped(part[1]) for part in (late, over)]
    others = [[part[:, begin:end] for part in whole] for begin, end in groups]
    middle_other, late[0] = lax.optimization_barrier((middle_other, late[0]))
    middle_other, middle_own = turn(middle_other, column, middle_own)

    (late, over, middle_own) = lax.optimization_barrier((late, over, middle_own))

    def added(a, b, here):
        return (a.astype(jnp.float32) + jnp.where(here, b.astype(jnp.float32), 0.0)).astype(jnp.bfloat16)

    out = None
    for (begin, end), (late_other, over_other) in zip(groups, others):

        def piece(way):
            mine = added(late[0][way, begin:end], over_other[way], block > 0)
            other = added(late_other[way], over[0][way, begin:end], block == 0)
            half = mine.shape[1] // 2
            return jnp.concatenate([mine[:, :half], other[:, :half], mine[:, half:], other[:, half:]], axis=1)

        tail = spread(piece)
        if end < own:
            came = [tail[way] for way in order[:4]]
            late, over, came = lax.optimization_barrier((late, over, came))
            for way, part in zip(order, came):
                tail[way] = part
        parts = [(early, begin), (middle_own, begin), (middle_other, begin), (tail, 0)]
        out = correlate(scale, spot, parts, out, begin, end - begin, own, chips, cores)
    return out


def solution(mesh):
    return jax.shard_map(
        local,
        mesh=mesh,
        in_specs=(
            P(("grp", "inp", "sub"), "tblk"),
            P(),
            P(("grp", "inp", "sub"), "tblk"),
            P("grp"),
            P(),
        ),
        out_specs=P(("grp", "inp", "tblk", "sub"), None, None),
        check_vma=False,
    )
```
